32 devices in a mesh: group: 2 (over y), ctx: 4 (over z), chan: 2 (over x), sub: 2 (over core).
Axes of the slice: x: 2, y: 2, z: 4, core: 2. Of those that a mesh axis runs over, the one named last changes fastest.
Arguments:
- q_proj: bfloat16 [2048, 4096], P(('group', 'ctx'), ('chan', 'sub')), parts along dimension 0, may hold values from -6 to 6
- k_proj: bfloat16 [2048, 4096], P(('group', 'ctx'), ('chan', 'sub')), parts along dimension 0, may hold values from -6 to 6
- v_proj: bfloat16 [2048, 4096], P(('group', 'ctx'), ('chan', 'sub')), parts along dimension 0, may hold values from -6 to 6
- filters: float32 [32, 512], P(('chan', 'sub')), may hold values from -0.375 to 0.375
- filter_blocks: int32 [32], P(('chan', 'sub')), may hold values from 1 to 2, as said below
- out_weight: bfloat16 [4096, 4096], P('ctx', ('chan', 'sub')), may hold values from -0.09375 to 0.09375
Outputs:
- mixed: bfloat16 [2048, 4096], P(('group', 'ctx'), ('chan', 'sub')), parts along dimension 0
The draws below stay inside these ranges and needn't reach their ends.
There are 2 independent parts, one for each index of `group`. The reference program is written for one: setup_inputs(seed, part) draws one part's arguments, and reference() takes and returns one part's arrays. A program takes and returns all parts, laid end to end along the dimension named above; an argument that names none is the same for every part. Nothing has to cross between parts.
Inputs may be any that keep to these rules, and one draw needn't show every extreme that they name: `filter_blocks`: some group has exactly the largest length.
All inputs are finite; a program needn't handle non-finite values.
Results may differ from the reference program's by a relative error of at most 0.0095.
Values may be sent and summed in bfloat16 or wider, within the bound.
No kernel may reach another device: no remote copies, remote signals or barrier semaphores. Data moves between devices by JAX's collectives and lax.ppermute only.
A program may use at most 64 MiB of HBM per device.

```python
import jax
import jax.numpy as jnp
from jax import lax

D = 4096
CPG = 128
BLK = 256
GROUPS = 32
MAXLEN = 2
SEQ = 1024


def draw_filter_blocks(key, part):
    key = jax.random.fold_in(key, 7)
    draw_key, spot_key = jax.random.split(key)
    lengths = jax.random.randint(draw_key, (GROUPS,), 1, MAXLEN + 1)
    longest_at = jax.random.randint(spot_key, (), 0, GROUPS)
    return jnp.where(jnp.arange(GROUPS) == longest_at, MAXLEN, lengths).astype(jnp.int32)


def block_scale(stream_key, dims, cuts, smallest, largest):
    loudness = 1.0
    for position, blocks in cuts:
        steps = jax.random.uniform(jax.random.fold_in(jax.random.fold_in(stream_key, 6), position), (blocks,), jnp.float32, smallest / len(cuts), largest / len(cuts))
        loudness = loudness * jnp.repeat(jnp.exp(steps), dims[position] // blocks).reshape((-1,) + (1,) * (len(dims) - 1 - position))
    return loudness


def gaussian(key, shape, scale, most, shards=(), held_as=jnp.bfloat16):
    result = jax.random.normal(key, shape, jnp.float32) * scale
    if len(shards) > 0:
        result = block_scale(key, shape, shards, -0.22, 0.18) * result
    return jnp.clip(result, min=-most, max=most).astype(held_as)


def setup_inputs(seed: int = 0, part: int = 0) -> dict:
    splits = jax.random.split(jax.random.key(seed), 7)
    own_keys = jax.random.split(jax.random.fold_in(splits[6], part), 7)
    q_proj = gaussian(own_keys[0], (SEQ, D), 1.0, 6.0, ((0, 4), (1, 4)))
    k_proj = gaussian(own_keys[1], (SEQ, D), 1.0, 6.0, ((0, 4), (1, 4)))
    v_proj = gaussian(own_keys[2], (SEQ, D), 1.0, 6.0, ((0, 4), (1, 4)))
    filters = gaussian(splits[3], (GROUPS, MAXLEN * BLK), ((MAXLEN * BLK) // 2) ** -0.5, 0.375, ((0, 4),), jnp.float32)
    filter_blocks = draw_filter_blocks(jax.random.fold_in(splits[6], 71), part)
    out_weight = gaussian(splits[5], (D, D), D ** -0.5, 0.09375, ((0, 4), (1, 4)))
    return {"q_proj": q_proj, "k_proj": k_proj, "v_proj": v_proj, "filters": filters, "filter_blocks": filter_blocks, "out_weight": out_weight}


def reference(q_proj, k_proj, v_proj, filters, filter_blocks, out_weight):
    product = (k_proj.astype(jnp.float32) * v_proj.astype(jnp.float32)).astype(jnp.bfloat16)
    tap_index = jnp.arange(filters.shape[1], dtype=jnp.int32)
    masked = jnp.where(tap_index[None, :] < filter_blocks[:, None] * BLK, filters, jnp.zeros_like(filters))
    grouped = product.astype(jnp.float32).reshape(SEQ, GROUPS, CPG).transpose(1, 0, 2)
    length = 2 * SEQ

    def per_group_conv(operands):
        signal, response = operands
        spectrum = jnp.fft.rfft(signal, n=length, axis=0)
        filter_spectrum = jnp.fft.rfft(response, n=length)
        return jnp.fft.irfft(spectrum * filter_spectrum[:, None], n=length, axis=0)[:SEQ]

    convolved = lax.map(per_group_conv, (grouped, masked))
    conv = convolved.transpose(1, 0, 2).reshape(SEQ, D).astype(jnp.float32)
    gated = (q_proj.astype(jnp.float32) * conv).astype(jnp.bfloat16)
    return jnp.dot(gated, out_weight, preferred_element_type=jnp.float32).astype(jnp.bfloat16)
```

```python
import math

import jax
import jax.numpy as jnp
from jax import lax
from jax.experimental import pallas as pl
from jax.experimental.pallas import tpu as pltpu
from jax.sharding import PartitionSpec as P


def shifted(value, axis, steps):
    count = lax.axis_size(axis)
    leading, last = (max(0, -steps), min(count, count - steps))
    return lax.ppermute(value, axis, [(source, source + steps) for source in range(leading, last)])


def forward_table(block_len, columns):
    length = 2 * block_len
    frequency = jnp.arange(block_len, dtype=jnp.int32)[:, None]
    positions = jnp.arange(columns, dtype=jnp.int32)[None, :]
    angles = (frequency * positions % length).astype(jnp.float32) * (2.0 * math.pi / length)
    alternating = (1 - 2 * (positions % 2)).astype(jnp.float32)
    upper = jnp.cos(angles)
    bottom = jnp.where(frequency == 0, alternating, -jnp.sin(angles))
    return jnp.concatenate([upper, bottom], axis=0)


def inverse_table(block_len):
    length = 2 * block_len
    samples = jnp.arange(block_len, dtype=jnp.int32)[:, None]
    frequency = jnp.arange(block_len, dtype=jnp.int32)[None, :]
    angles = (frequency * samples % length).astype(jnp.float32) * (2.0 * math.pi / length)
    alternating = (1 - 2 * (samples % 2)).astype(jnp.float32)
    left_half = jnp.where(frequency == 0, 1.0, 2.0 * jnp.cos(angles)) / length
    right_half = jnp.where(frequency == 0, alternating, -2.0 * jnp.sin(angles)) / length
    return jnp.concatenate([left_half, right_half], axis=1)


def packed_product(filter_spec, data_spec, first_row, block_len):
    filt_re = filter_spec[:block_len]
    filt_im = filter_spec[block_len:]
    data_re = data_spec[:block_len]
    data_im = data_spec[block_len:]
    other_rows = 1.0 - first_row
    upper = filt_re * data_re - filt_im * data_im * other_rows
    bottom = (filt_re * data_im + filt_im * data_re) * other_rows + filt_im * data_im * first_row
    return jnp.concatenate([upper, bottom], axis=0)


def gathered_plan(q_proj, k_proj, v_proj, filters, filter_blocks, out_weight):
    block_len, channels = q_proj.shape
    groups = filters.shape[0]
    per_group = channels // groups
    reach = lax.axis_size("ctx") // 2
    highest = lax.Precision.HIGHEST
    product = (k_proj.astype(jnp.float32) * v_proj.astype(jnp.float32)).astype(jnp.bfloat16)
    tap_index = jnp.arange(filters.shape[1], dtype=jnp.int32)
    masked = jnp.where(tap_index[None, :] < filter_blocks[:, None] * block_len, filters, 0.0)
    tap_blocks = masked.reshape(groups, reach, block_len)
    empty_block = jnp.zeros((groups, 1, block_len), jnp.float32)
    extended = jnp.concatenate([empty_block, tap_blocks, empty_block], axis=1)
    segments = jnp.concatenate([extended[:, 1:], extended[:, :-1]], axis=2)
    full_table = forward_table(block_len, 2 * block_len)
    filter_spectra = jnp.einsum("gdm,fm->dfg", segments, full_table, precision=highest)
    half_table = forward_table(block_len, block_len)
    table_high = half_table.astype(jnp.bfloat16)
    table_low = (half_table - table_high.astype(jnp.float32)).astype(jnp.bfloat16)
    first_row = (jnp.arange(block_len) == 0).astype(jnp.float32)[:, None, None]
    longest = jnp.max(filter_blocks)
    position = lax.axis_index("ctx")

    def transform(block):
        spectrum = jnp.dot(table_high, block, preferred_element_type=jnp.float32)
        spectrum = spectrum + jnp.dot(table_low, block, preferred_element_type=jnp.float32)
        return spectrum.reshape(2 * block_len, groups, per_group)

    def contribution(running, block, distance):
        filter_spec = lax.dynamic_index_in_dim(filter_spectra, distance, 0, keepdims=False)[
            :, :, None
        ]

        def add_term(partial_sum):
            return partial_sum + packed_product(filter_spec, transform(block), first_row, block_len)

        needed = (distance <= longest) & (position >= distance)
        return lax.cond(needed, add_term, lambda partial_sum: partial_sum, running)

    running = packed_product(
        filter_spectra[0][:, :, None], transform(product), first_row, block_len
    )

    def relay_step(distance, carry):
        carried, partial_sum = carry
        carried = shifted(carried, "ctx", 1)
        return (carried, contribution(partial_sum, carried, distance))

    carried, running = lax.fori_loop(1, reach + 1, relay_step, (product, running))
    spectrum_sum = running.reshape(2 * block_len, channels)
    conv = jnp.dot(inverse_table(block_len), spectrum_sum, precision=highest)
    gated = (q_proj.astype(jnp.float32) * conv).astype(jnp.bfloat16)
    all_gated = lax.all_gather(gated, ("chan", "sub"), axis=1, tiled=True)
    mixed = jnp.dot(
        all_gated,
        lax.all_gather(out_weight, "ctx", axis=0, tiled=True),
        preferred_element_type=jnp.float32,
    )
    return mixed.astype(jnp.bfloat16)


def swap(value, *axes):
    sizes = [lax.axis_size(axis) for axis in axes]
    total = math.prod(sizes)
    flip, stride = 0, 1
    for size in reversed(sizes):
        flip += stride
        stride *= size
    return lax.ppermute(value, axes, [(i, i ^ flip) for i in range(total)])


def across(value, distance):
    count = lax.axis_size("ctx")
    return lax.ppermute(value, "ctx", [(i, i ^ distance) for i in range(count)])


def conv_kernel(place, row_ref, *refs):
    pieces, conv_ref, padded = refs[:4], refs[4], refs[5]
    block, width = pieces[0].shape
    groups, span = row_ref.shape
    per_group = width // groups
    padded[0] = jnp.zeros((block, width), padded.dtype)
    padded[1] = jnp.zeros((block, width), padded.dtype)
    for distance in range(4):
        padded[2 + (place[0] ^ distance)] = pieces[distance][...]
    for group in range(groups):
        columns = pl.ds(group * per_group, per_group)
        rows = jnp.broadcast_to(row_ref[group : group + 1, :], (block, span))
        toeplitz = pltpu.roll(rows, 0, 1, stride=1, stride_axis=0).astype(jnp.bfloat16)
        for token in range(4):
            source = jnp.concatenate([padded[token + step, :, columns] for step in range(3)], axis=0)
            conv_ref[token, :, columns] = jnp.dot(
                toeplitz, source, preferred_element_type=jnp.float32
            )


def causal_conv(place, first_rows, pieces):
    block, width = pieces[0].shape
    return pl.pallas_call(
        conv_kernel,
        out_shape=jax.ShapeDtypeStruct((4, block, width), jnp.float32),
        grid_spec=pltpu.PrefetchScalarGridSpec(
            num_scalar_prefetch=1,
            grid=(1,),
            in_specs=[pl.BlockSpec(first_rows.shape, lambda i, s: (0, 0))]
            + [pl.BlockSpec((block, width), lambda i, s: (0, 0))] * 4,
            out_specs=pl.BlockSpec((4, block, width), lambda i, s: (0, 0, 0)),
            scratch_shapes=[pltpu.VMEM((6, block, width), jnp.bfloat16)],
        ),
        compiler_params=pltpu.CompilerParams(vmem_limit_bytes=32 * 2**20),
        cost_estimate=pl.CostEstimate(
            flops=2 * 4 * block * 3 * block * width, bytes_accessed=2**21, transcendentals=0
        ),
    )(place, first_rows, *pieces)


def project_kernel(place, *refs):
    mine, other, own_w, got_w, out_ref = refs[:4], refs[4], refs[5], refs[6], refs[7]
    bit, quarter, same = place[1], place[2], place[3]
    tokens, width = mine[0].shape
    half = tokens // 2
    for part in range(2):
        rows = pl.ds(part * half, half)
        total = jnp.zeros((half, out_ref.shape[2]), jnp.float32)
        for flip in range(4):
            here, there = mine[flip][rows, :], other[flip, rows, :]
            first = jnp.where(same == 1, here, there)
            second = jnp.where(same == 1, there, here)
            block = pl.ds(pl.multiple_of((quarter ^ flip) * width, width), width)
            total += jnp.dot(first, own_w[block, :], preferred_element_type=jnp.float32)
            total += jnp.dot(second, got_w[block, :], preferred_element_type=jnp.float32)
        out_ref[part ^ bit] = total.astype(out_ref.dtype)


def project(place, mine, other, out_weight, got_w):
    tokens, width = mine[0].shape
    depth, columns = got_w.shape
    return pl.pallas_call(
        project_kernel,
        out_shape=jax.ShapeDtypeStruct((2, tokens // 2, columns), jnp.bfloat16),
        grid_spec=pltpu.PrefetchScalarGridSpec(
            num_scalar_prefetch=1,
            grid=(1,),
            in_specs=[pl.BlockSpec((tokens, width), lambda i, s: (0, 0))] * 4
            + [
                pl.BlockSpec((4, tokens, width), lambda i, s: (0, 0, 0)),
                pl.BlockSpec((depth, columns), lambda i, s: (0, s[1])),
                pl.BlockSpec((depth, columns), lambda i, s: (0, 0)),
            ],
            out_specs=pl.BlockSpec((2, tokens // 2, columns), lambda i, s: (0, 0, 0)),
        ),
        compiler_params=pltpu.CompilerParams(vmem_limit_bytes=32 * 2**20),
        cost_estimate=pl.CostEstimate(
            flops=2 * tokens * 8 * width * columns, bytes_accessed=2**22, transcendentals=0
        ),
    )(place, *mine, other, out_weight, got_w)


def paired_plan(q_proj, k_proj, v_proj, filters, filter_blocks, out_weight):
    block, channels = q_proj.shape
    groups = filters.shape[0]
    z, x, c = lax.axis_index("ctx"), lax.axis_index("chan"), lax.axis_index("sub")
    pair, bit = z // 2, z % 2
    quarter = 2 * x + bit
    half, fourth = channels // 2, channels // 4
    place = jnp.stack([z, bit, quarter, (c == bit).astype(jnp.int32)]).astype(jnp.int32)

    tap_index = jnp.arange(filters.shape[1], dtype=jnp.int32)
    masked = jnp.where(tap_index[None, :] < filter_blocks[:, None] * block, filters, 0.0)
    taken = groups // 4
    for_other = lax.dynamic_slice_in_dim(masked, (2 * (1 - x) + bit) * taken, taken, 0)
    taps = jnp.where(
        pair == x, lax.dynamic_slice_in_dim(masked, quarter * taken, taken, 0), swap(for_other, "chan")
    )
    first_rows = jnp.concatenate(
        [jnp.zeros((taken, 1), jnp.float32), taps[:, ::-1], jnp.zeros((taken, block - 1), jnp.float32)],
        axis=1,
    )

    product = (k_proj.astype(jnp.float32) * v_proj.astype(jnp.float32)).astype(jnp.bfloat16)

    def spread(array):
        kept = lax.dynamic_slice_in_dim(array, x * half, half, 1)
        came = swap(lax.dynamic_slice_in_dim(array, (1 - x) * half, half, 1), "chan")
        pieces = []
        for distance in range(4):
            target = z ^ distance
            start = (target % 2) * fourth
            pieces.append(
                jnp.where(
                    target // 2 == x,
                    lax.dynamic_slice_in_dim(kept, start, fourth, 1),
                    lax.dynamic_slice_in_dim(came, start, fourth, 1),
                )
            )
        return [pieces[0]] + [across(pieces[distance], distance) for distance in (1, 2, 3)]

    product_pieces = spread(product)
    q_pieces = spread(q_proj)
    got_w = across(lax.dynamic_slice_in_dim(out_weight, (1 - bit) * half, half, 1), 1)
    conv = causal_conv(place, first_rows, product_pieces)

    def mixed_partials(own, near, which):
        low = jnp.where(bit == 0, own, near)
        high = jnp.where(bit == 0, near, own)
        gate = jnp.stack([low, high])
        signal = lax.dynamic_slice_in_dim(conv, 2 * which, 2, 0)
        gated = (gate.astype(jnp.float32) * signal).astype(jnp.bfloat16).reshape(2 * block, fourth)
        mine = [gated, swap(gated, "ctx"), swap(gated, "chan"), swap(gated, "ctx", "chan")]
        other = swap(jnp.stack(mine), "sub")
        return project(place, mine, other, out_weight, got_w)

    far = mixed_partials(q_pieces[2], q_pieces[3], 1 - pair)
    far_own, far_near = across(far[0], 2), across(far[1], 3)
    close = mixed_partials(q_pieces[0], q_pieces[1], pair)
    near = across(close[1], 1)
    this_half = close[0].astype(jnp.float32) + far_own.astype(jnp.float32)
    that_half = near.astype(jnp.float32) + far_near.astype(jnp.float32)
    left = jnp.where(bit == 0, this_half, that_half)
    right = jnp.where(bit == 0, that_half, this_half)
    return jnp.concatenate([left, right], axis=1).astype(jnp.bfloat16)


def solution(mesh):
    sizes = dict(mesh.shape)

    def per_device(q_proj, k_proj, v_proj, filters, filter_blocks, out_weight):
        block, channels = q_proj.shape
        groups, taps = filters.shape
        paired = (
            (sizes["ctx"], sizes["chan"], sizes["sub"]) == (4, 2, 2)
            and taps == 2 * block
            and groups % 4 == 0
            and (channels // groups) % 128 == 0
            and out_weight.shape == (channels, channels)
        )
        plan = paired_plan if paired else gathered_plan
        return plan(q_proj, k_proj, v_proj, filters, filter_blocks, out_weight)

    in_specs = (
        P(("group", "ctx"), ("chan", "sub")),
        P(("group", "ctx"), ("chan", "sub")),
        P(("group", "ctx"), ("chan", "sub")),
        P(("chan", "sub"), None),
        P(("chan", "sub")),
        P("ctx", ("chan", "sub")),
    )
    out_specs = P(("group", "ctx"), ("chan", "sub"))
    return jax.shard_map(
        per_device, mesh=mesh, in_specs=in_specs, out_specs=out_specs, check_vma=False
    )
```

```python
import math

import jax
import jax.numpy as jnp
from jax import lax
from jax.experimental import pallas as pl
from jax.experimental.pallas import tpu as pltpu
from jax.sharding import PartitionSpec as P


def shifted(value, axis, steps):
    count = lax.axis_size(axis)
    leading, last = (max(0, -steps), min(count, count - steps))
    return lax.ppermute(value, axis, [(source, source + steps) for source in range(leading, last)])


def forward_table(block_len, columns):
    length = 2 * block_len
    frequency = jnp.arange(block_len, dtype=jnp.int32)[:, None]
    positions = jnp.arange(columns, dtype=jnp.int32)[None, :]
    angles = (frequency * positions % length).astype(jnp.float32) * (2.0 * math.pi / length)
    alternating = (1 - 2 * (positions % 2)).astype(jnp.float32)
    upper = jnp.cos(angles)
    bottom = jnp.where(frequency == 0, alternating, -jnp.sin(angles))
    return jnp.concatenate([upper, bottom], axis=0)


def inverse_table(block_len):
    length = 2 * block_len
    samples = jnp.arange(block_len, dtype=jnp.int32)[:, None]
    frequency = jnp.arange(block_len, dtype=jnp.int32)[None, :]
    angles = (frequency * samples % length).astype(jnp.float32) * (2.0 * math.pi / length)
    alternating = (1 - 2 * (samples % 2)).astype(jnp.float32)
    left_half = jnp.where(frequency == 0, 1.0, 2.0 * jnp.cos(angles)) / length
    right_half = jnp.where(frequency == 0, alternating, -2.0 * jnp.sin(angles)) / length
    return jnp.concatenate([left_half, right_half], axis=1)


def packed_product(filter_spec, data_spec, first_row, block_len):
    filt_re = filter_spec[:block_len]
    filt_im = filter_spec[block_len:]
    data_re = data_spec[:block_len]
    data_im = data_spec[block_len:]
    other_rows = 1.0 - first_row
    upper = filt_re * data_re - filt_im * data_im * other_rows
    bottom = (filt_re * data_im + filt_im * data_re) * other_rows + filt_im * data_im * first_row
    return jnp.concatenate([upper, bottom], axis=0)


def gathered_plan(q_proj, k_proj, v_proj, filters, filter_blocks, out_weight):
    block_len, channels = q_proj.shape
    groups = filters.shape[0]
    per_group = channels // groups
    reach = lax.axis_size("ctx") // 2
    highest = lax.Precision.HIGHEST
    product = (k_proj.astype(jnp.float32) * v_proj.astype(jnp.float32)).astype(jnp.bfloat16)
    tap_index = jnp.arange(filters.shape[1], dtype=jnp.int32)
    masked = jnp.where(tap_index[None, :] < filter_blocks[:, None] * block_len, filters, 0.0)
    tap_blocks = masked.reshape(groups, reach, block_len)
    empty_block = jnp.zeros((groups, 1, block_len), jnp.float32)
    extended = jnp.concatenate([empty_block, tap_blocks, empty_block], axis=1)
    segments = jnp.concatenate([extended[:, 1:], extended[:, :-1]], axis=2)
    full_table = forward_table(block_len, 2 * block_len)
    filter_spectra = jnp.einsum("gdm,fm->dfg", segments, full_table, precision=highest)
    half_table = forward_table(block_len, block_len)
    table_high = half_table.astype(jnp.bfloat16)
    table_low = (half_table - table_high.astype(jnp.float32)).astype(jnp.bfloat16)
    first_row = (jnp.arange(block_len) == 0).astype(jnp.float32)[:, None, None]
    longest = jnp.max(filter_blocks)
    position = lax.axis_index("ctx")

    def transform(block):
        spectrum = jnp.dot(table_high, block, preferred_element_type=jnp.float32)
        spectrum = spectrum + jnp.dot(table_low, block, preferred_element_type=jnp.float32)
        return spectrum.reshape(2 * block_len, groups, per_group)

    def contribution(running, block, distance):
        filter_spec = lax.dynamic_index_in_dim(filter_spectra, distance, 0, keepdims=False)[
            :, :, None
        ]

        def add_term(partial_sum):
            return partial_sum + packed_product(filter_spec, transform(block), first_row, block_len)

        needed = (distance <= longest) & (position >= distance)
        return lax.cond(needed, add_term, lambda partial_sum: partial_sum, running)

    running = packed_product(
        filter_spectra[0][:, :, None], transform(product), first_row, block_len
    )

    def relay_step(distance, carry):
        carried, partial_sum = carry
        carried = shifted(carried, "ctx", 1)
        return (carried, contribution(partial_sum, carried, distance))

    carried, running = lax.fori_loop(1, reach + 1, relay_step, (product, running))
    spectrum_sum = running.reshape(2 * block_len, channels)
    conv = jnp.dot(inverse_table(block_len), spectrum_sum, precision=highest)
    gated = (q_proj.astype(jnp.float32) * conv).astype(jnp.bfloat16)
    all_gated = lax.all_gather(gated, ("chan", "sub"), axis=1, tiled=True)
    mixed = jnp.dot(
        all_gated,
        lax.all_gather(out_weight, "ctx", axis=0, tiled=True),
        preferred_element_type=jnp.float32,
    )
    return mixed.astype(jnp.bfloat16)


def swap(value, *axes):
    sizes = [lax.axis_size(axis) for axis in axes]
    total = math.prod(sizes)
    flip, stride = 0, 1
    for size in reversed(sizes):
        flip += stride
        stride *= size
    return lax.ppermute(value, axes, [(i, i ^ flip) for i in range(total)])


def across(value, distance):
    count = lax.axis_size("ctx")
    return lax.ppermute(value, "ctx", [(i, i ^ distance) for i in range(count)])


def conv_kernel(place, row_ref, *refs):
    pieces, conv_ref, padded = refs[:4], refs[4], refs[5]
    block, width = pieces[0].shape
    groups, span = row_ref.shape
    per_group = width // groups
    padded[0] = jnp.zeros((block, width), padded.dtype)
    padded[1] = jnp.zeros((block, width), padded.dtype)
    for distance in range(4):
        padded[2 + (place[0] ^ distance)] = pieces[distance][...]
    for group in range(groups):
        columns = pl.ds(group * per_group, per_group)
        rows = jnp.broadcast_to(row_ref[group : group + 1, :], (block, span))
        toeplitz = pltpu.roll(rows, 0, 1, stride=1, stride_axis=0).astype(jnp.bfloat16)
        for token in range(4):
            source = jnp.concatenate([padded[token + step, :, columns] for step in range(3)], axis=0)
            conv_ref[token, :, columns] = jnp.dot(
                toeplitz, source, preferred_element_type=jnp.float32
            )


def causal_conv(place, first_rows, pieces):
    block, width = pieces[0].shape
    return pl.pallas_call(
        conv_kernel,
        out_shape=jax.ShapeDtypeStruct((4, block, width), jnp.float32),
        grid_spec=pltpu.PrefetchScalarGridSpec(
            num_scalar_prefetch=1,
            grid=(1,),
            in_specs=[pl.BlockSpec(first_rows.shape, lambda i, s: (0, 0))]
            + [pl.BlockSpec((block, width), lambda i, s: (0, 0))] * 4,
            out_specs=pl.BlockSpec((4, block, width), lambda i, s: (0, 0, 0)),
            scratch_shapes=[pltpu.VMEM((6, block, width), jnp.bfloat16)],
        ),
        compiler_params=pltpu.CompilerParams(vmem_limit_bytes=32 * 2**20),
        cost_estimate=pl.CostEstimate(
            flops=2 * 4 * block * 3 * block * width, bytes_accessed=2**21, transcendentals=0
        ),
    )(place, first_rows, *pieces)


def project_kernel(place, *refs):
    mine, other, own_w, got_w, out_ref = refs[:4], refs[4], refs[5], refs[6], refs[7]
    bit, quarter, same = place[1], place[2], place[3]
    tokens, width = mine[0].shape
    half = tokens // 2
    for part in range(2):
        rows = pl.ds(part * half, half)
        total = jnp.zeros((half, out_ref.shape[2]), jnp.float32)
        for flip in range(4):
            here, there = mine[flip][rows, :], other[flip, rows, :]
            first = jnp.where(same == 1, here, there)
            second = jnp.where(same == 1, there, here)
            block = pl.ds(pl.multiple_of((quarter ^ flip) * width, width), width)
            total += jnp.dot(first, own_w[block, :], preferred_element_type=jnp.float32)
            total += jnp.dot(second, got_w[block, :], preferred_element_type=jnp.float32)
        out_ref[part ^ bit] = total.astype(out_ref.dtype)


def project(place, mine, other, out_weight, got_w):
    tokens, width = mine[0].shape
    depth, columns = got_w.shape
    return pl.pallas_call(
        project_kernel,
        out_shape=jax.ShapeDtypeStruct((2, tokens // 2, columns), jnp.bfloat16),
        grid_spec=pltpu.PrefetchScalarGridSpec(
            num_scalar_prefetch=1,
            grid=(1,),
            in_specs=[pl.BlockSpec((tokens, width), lambda i, s: (0, 0))] * 4
            + [
                pl.BlockSpec((4, tokens, width), lambda i, s: (0, 0, 0)),
                pl.BlockSpec((depth, columns), lambda i, s: (0, s[1])),
                pl.BlockSpec((depth, columns), lambda i, s: (0, 0)),
            ],
            out_specs=pl.BlockSpec((2, tokens // 2, columns), lambda i, s: (0, 0, 0)),
        ),
        compiler_params=pltpu.CompilerParams(vmem_limit_bytes=32 * 2**20),
        cost_estimate=pl.CostEstimate(
            flops=2 * tokens * 8 * width * columns, bytes_accessed=2**22, transcendentals=0
        ),
    )(place, *mine, other, out_weight, got_w)


def paired_plan(q_proj, k_proj, v_proj, filters, filter_blocks, out_weight):
    block, channels = q_proj.shape
    groups = filters.shape[0]
    z, x, c = lax.axis_index("ctx"), lax.axis_index("chan"), lax.axis_index("sub")
    g = lax.axis_index("group")
    pair, bit = z // 2, z % 2
    quarter = 2 * x + bit
    half, fourth = channels // 2, channels // 4
    place = jnp.stack([z, bit, quarter, (c == bit).astype(jnp.int32)]).astype(jnp.int32)

    other_cols = (1 - bit) * half + g * fourth
    w_near = across(lax.dynamic_slice_in_dim(out_weight, other_cols, fourth, 1), 1)
    w_far = swap(w_near, "group")
    got_w = jnp.where(
        g == 0, jnp.concatenate([w_near, w_far], axis=1), jnp.concatenate([w_far, w_near], axis=1)
    )

    tap_index = jnp.arange(filters.shape[1], dtype=jnp.int32)
    masked = jnp.where(tap_index[None, :] < filter_blocks[:, None] * block, filters, 0.0)
    masked = masked.astype(jnp.bfloat16)
    taken = groups // 4
    for_other = lax.dynamic_slice_in_dim(masked, (2 * (1 - x) + bit) * taken, taken, 0)
    for_other = jnp.concatenate([for_other, jnp.zeros((16 - taken, half), jnp.bfloat16)], axis=0)

    product = (k_proj.astype(jnp.float32) * v_proj.astype(jnp.float32)).astype(jnp.bfloat16)
    product_send = lax.dynamic_slice_in_dim(product, (1 - x) * half, half, 1)
    came = swap(jnp.concatenate([product_send, for_other], axis=0), "chan")
    taps = jnp.where(
        pair == x, lax.dynamic_slice_in_dim(masked, quarter * taken, taken, 0), came[block : block + taken]
    ).astype(jnp.float32)
    first_rows = jnp.concatenate(
        [jnp.zeros((taken, 1), jnp.float32), taps[:, ::-1], jnp.zeros((taken, block - 1), jnp.float32)],
        axis=1,
    )

    def spread(array, came):
        kept = lax.dynamic_slice_in_dim(array, x * half, half, 1)
        pieces = []
        for distance in range(4):
            target = z ^ distance
            start = (target % 2) * fourth
            pieces.append(
                jnp.where(
                    target // 2 == x,
                    lax.dynamic_slice_in_dim(kept, start, fourth, 1),
                    lax.dynamic_slice_in_dim(came[:block], start, fourth, 1),
                )
            )
        return [pieces[0]] + [across(pieces[distance], distance) for distance in (1, 2, 3)]

    product_pieces = spread(product, came)
    q_pieces = spread(
        q_proj, swap(lax.dynamic_slice_in_dim(q_proj, (1 - x) * half, half, 1), "chan")
    )
    first_rows, got_w = lax.optimization_barrier((first_rows, got_w))
    conv = causal_conv(place, first_rows, product_pieces)

    def mixed_partials(own, near, which):
        low = jnp.where(bit == 0, own, near)
        high = jnp.where(bit == 0, near, own)
        gate = jnp.stack([low, high])
        signal = lax.dynamic_slice_in_dim(conv, 2 * which, 2, 0)
        gated = (gate.astype(jnp.float32) * signal).astype(jnp.bfloat16).reshape(2 * block, fourth)
        mine = [gated, swap(gated, "ctx"), swap(gated, "chan"), swap(gated, "ctx", "chan")]
        other = swap(jnp.stack(mine), "sub")
        return project(place, mine, other, out_weight, got_w)

    far = mixed_partials(q_pieces[2], q_pieces[3], 1 - pair)
    far_own, far_near = across(far[0], 2), across(far[1], 3)
    close = mixed_partials(q_pieces[0], q_pieces[1], pair)
    near = across(close[1], 1)
    this_half = close[0].astype(jnp.float32) + far_own.astype(jnp.float32)
    that_half = near.astype(jnp.float32) + far_near.astype(jnp.float32)
    left = jnp.where(bit == 0, this_half, that_half)
    right = jnp.where(bit == 0, that_half, this_half)
    return jnp.concatenate([left, right], axis=1).astype(jnp.bfloat16)


def solution(mesh):
    sizes = dict(mesh.shape)

    def per_device(q_proj, k_proj, v_proj, filters, filter_blocks, out_weight):
        block, channels = q_proj.shape
        groups, taps = filters.shape
        paired = (
            (sizes["group"], sizes["ctx"], sizes["chan"], sizes["sub"]) == (2, 4, 2, 2)
            and taps == 2 * block
            and taps == channels // 2
            and groups % 4 == 0
            and (channels // groups) % 128 == 0
            and out_weight.shape == (channels, channels)
        )
        plan = paired_plan if paired else gathered_plan
        return plan(q_proj, k_proj, v_proj, filters, filter_blocks, out_weight)

    in_specs = (
        P(("group", "ctx"), ("chan", "sub")),
        P(("group", "ctx"), ("chan", "sub")),
        P(("group", "ctx"), ("chan", "sub")),
        P(("chan", "sub"), None),
        P(("chan", "sub")),
        P("ctx", ("chan", "sub")),
    )
    out_specs = P(("group", "ctx"), ("chan", "sub"))
    return jax.shard_map(
        per_device, mesh=mesh, in_specs=in_specs, out_specs=out_specs, check_vma=False
    )
```

```python
import math

import jax
import jax.numpy as jnp
from jax import lax
from jax.experimental import pallas as pl
from jax.experimental.pallas import tpu as pltpu
from jax.sharding import PartitionSpec as P


def shifted(value, axis, steps):
    count = lax.axis_size(axis)
    leading, last = (max(0, -steps), min(count, count - steps))
    return lax.ppermute(value, axis, [(source, source + steps) for source in range(leading, last)])


def forward_table(block_len, columns):
    length = 2 * block_len
    frequency = jnp.arange(block_len, dtype=jnp.int32)[:, None]
    positions = jnp.arange(columns, dtype=jnp.int32)[None, :]
    angles = (frequency * positions % length).astype(jnp.float32) * (2.0 * math.pi / length)
    alternating = (1 - 2 * (positions % 2)).astype(jnp.float32)
    upper = jnp.cos(angles)
    bottom = jnp.where(frequency == 0, alternating, -jnp.sin(angles))
    return jnp.concatenate([upper, bottom], axis=0)


def inverse_table(block_len):
    length = 2 * block_len
    samples = jnp.arange(block_len, dtype=jnp.int32)[:, None]
    frequency = jnp.arange(block_len, dtype=jnp.int32)[None, :]
    angles = (frequency * samples % length).astype(jnp.float32) * (2.0 * math.pi / length)
    alternating = (1 - 2 * (samples % 2)).astype(jnp.float32)
    left_half = jnp.where(frequency == 0, 1.0, 2.0 * jnp.cos(angles)) / length
    right_half = jnp.where(frequency == 0, alternating, -2.0 * jnp.sin(angles)) / length
    return jnp.concatenate([left_half, right_half], axis=1)


def packed_product(filter_spec, data_spec, first_row, block_len):
    filt_re = filter_spec[:block_len]
    filt_im = filter_spec[block_len:]
    data_re = data_spec[:block_len]
    data_im = data_spec[block_len:]
    other_rows = 1.0 - first_row
    upper = filt_re * data_re - filt_im * data_im * other_rows
    bottom = (filt_re * data_im + filt_im * data_re) * other_rows + filt_im * data_im * first_row
    return jnp.concatenate([upper, bottom], axis=0)


def gathered_plan(q_proj, k_proj, v_proj, filters, filter_blocks, out_weight):
    block_len, channels = q_proj.shape
    groups = filters.shape[0]
    per_group = channels // groups
    reach = lax.axis_size("ctx") // 2
    highest = lax.Precision.HIGHEST
    product = (k_proj.astype(jnp.float32) * v_proj.astype(jnp.float32)).astype(jnp.bfloat16)
    tap_index = jnp.arange(filters.shape[1], dtype=jnp.int32)
    masked = jnp.where(tap_index[None, :] < filter_blocks[:, None] * block_len, filters, 0.0)
    tap_blocks = masked.reshape(groups, reach, block_len)
    empty_block = jnp.zeros((groups, 1, block_len), jnp.float32)
    extended = jnp.concatenate([empty_block, tap_blocks, empty_block], axis=1)
    segments = jnp.concatenate([extended[:, 1:], extended[:, :-1]], axis=2)
    full_table = forward_table(block_len, 2 * block_len)
    filter_spectra = jnp.einsum("gdm,fm->dfg", segments, full_table, precision=highest)
    half_table = forward_table(block_len, block_len)
    table_high = half_table.astype(jnp.bfloat16)
    table_low = (half_table - table_high.astype(jnp.float32)).astype(jnp.bfloat16)
    first_row = (jnp.arange(block_len) == 0).astype(jnp.float32)[:, None, None]
    longest = jnp.max(filter_blocks)
    position = lax.axis_index("ctx")

    def transform(block):
        spectrum = jnp.dot(table_high, block, preferred_element_type=jnp.float32)
        spectrum = spectrum + jnp.dot(table_low, block, preferred_element_type=jnp.float32)
        return spectrum.reshape(2 * block_len, groups, per_group)

    def contribution(running, block, distance):
        filter_spec = lax.dynamic_index_in_dim(filter_spectra, distance, 0, keepdims=False)[
            :, :, None
        ]

        def add_term(partial_sum):
            return partial_sum + packed_product(filter_spec, transform(block), first_row, block_len)

        needed = (distance <= longest) & (position >= distance)
        return lax.cond(needed, add_term, lambda partial_sum: partial_sum, running)

    running = packed_product(
        filter_spectra[0][:, :, None], transform(product), first_row, block_len
    )

    def relay_step(distance, carry):
        carried, partial_sum = carry
        carried = shifted(carried, "ctx", 1)
        return (carried, contribution(partial_sum, carried, distance))

    carried, running = lax.fori_loop(1, reach + 1, relay_step, (product, running))
    spectrum_sum = running.reshape(2 * block_len, channels)
    conv = jnp.dot(inverse_table(block_len), spectrum_sum, precision=highest)
    gated = (q_proj.astype(jnp.float32) * conv).astype(jnp.bfloat16)
    all_gated = lax.all_gather(gated, ("chan", "sub"), axis=1, tiled=True)
    mixed = jnp.dot(
        all_gated,
        lax.all_gather(out_weight, "ctx", axis=0, tiled=True),
        preferred_element_type=jnp.float32,
    )
    return mixed.astype(jnp.bfloat16)


def swap(value, *axes):
    sizes = [lax.axis_size(axis) for axis in axes]
    total = math.prod(sizes)
    flip, stride = 0, 1
    for size in reversed(sizes):
        flip += stride
        stride *= size
    return lax.ppermute(value, axes, [(i, i ^ flip) for i in range(total)])


def across(value, distance):
    count = lax.axis_size("ctx")
    return lax.ppermute(value, "ctx", [(i, i ^ distance) for i in range(count)])


def gated_kernel(place, row_ref, *refs):
    pieces, outs, padded, gates = refs[:4], refs[4:6], refs[6], refs[7]
    _, block, width = pieces[0].shape
    groups, span = row_ref.shape
    per_group = width // groups
    padded[0] = jnp.zeros((block, width), padded.dtype)
    padded[1] = jnp.zeros((block, width), padded.dtype)
    for distance in range(4):
        token = place[0] ^ distance
        padded[2 + token] = pieces[distance][0]
        gates[token] = pieces[distance][1]
    for group in range(groups):
        columns = pl.ds(group * per_group, per_group)
        rows = jnp.broadcast_to(row_ref[group : group + 1, :], (block, span))
        toeplitz = pltpu.roll(rows, 0, 1, stride=1, stride_axis=0).astype(jnp.bfloat16)
        for out_ref, pair in zip(outs, (1 - place[4], place[4])):
            for part in range(2):
                token = 2 * pair + part
                source = jnp.concatenate(
                    [padded[token + step, :, columns] for step in range(3)], axis=0
                )
                conv = jnp.dot(toeplitz, source, preferred_element_type=jnp.float32)
                gated = gates[token, :, columns].astype(jnp.float32) * conv
                out_ref[pl.ds(part * block, block), columns] = gated.astype(out_ref.dtype)


def gated_conv(place, first_rows, pieces):
    _, block, width = pieces[0].shape
    return pl.pallas_call(
        gated_kernel,
        out_shape=[jax.ShapeDtypeStruct((2 * block, width), jnp.bfloat16)] * 2,
        grid_spec=pltpu.PrefetchScalarGridSpec(
            num_scalar_prefetch=1,
            grid=(1,),
            in_specs=[pl.BlockSpec(first_rows.shape, lambda i, s: (0, 0))]
            + [pl.BlockSpec((2, block, width), lambda i, s: (0, 0, 0))] * 4,
            out_specs=[pl.BlockSpec((2 * block, width), lambda i, s: (0, 0))] * 2,
            scratch_shapes=[
                pltpu.VMEM((6, block, width), jnp.bfloat16),
                pltpu.VMEM((4, block, width), jnp.bfloat16),
            ],
        ),
        compiler_params=pltpu.CompilerParams(vmem_limit_bytes=32 * 2**20),
        cost_estimate=pl.CostEstimate(
            flops=2 * 4 * block * 3 * block * width, bytes_accessed=2**21, transcendentals=0
        ),
    )(place, first_rows, *pieces)


def project_kernel(place, *refs):
    mine, other, own_w, near_w, far_w, out_ref = refs[:4], *refs[4:9]
    bit, quarter, same, group = place[1], place[2], place[3], place[5]
    tokens, width = mine[0].shape
    half = tokens // 2
    columns = near_w.shape[1]
    for part in range(2):
        rows = pl.ds(part * half, half)
        for got_w, index in ((near_w, group), (far_w, 1 - group)):
            place_of = pl.ds(pl.multiple_of(index * columns, columns), columns)
            total = jnp.zeros((half, columns), jnp.float32)
            for flip in range(4):
                here, there = mine[flip][rows, :], other[flip, rows, :]
                first = jnp.where(same == 1, here, there)
                second = jnp.where(same == 1, there, here)
                block = pl.ds(pl.multiple_of((quarter ^ flip) * width, width), width)
                total += jnp.dot(first, own_w[block, place_of], preferred_element_type=jnp.float32)
                total += jnp.dot(second, got_w[block, :], preferred_element_type=jnp.float32)
            out_ref[part ^ bit, :, place_of] = total.astype(out_ref.dtype)


def project(place, mine, other, out_weight, near_w, far_w):
    tokens, width = mine[0].shape
    depth, columns = near_w.shape
    return pl.pallas_call(
        project_kernel,
        out_shape=jax.ShapeDtypeStruct((2, tokens // 2, 2 * columns), jnp.bfloat16),
        grid_spec=pltpu.PrefetchScalarGridSpec(
            num_scalar_prefetch=1,
            grid=(1,),
            in_specs=[pl.BlockSpec((tokens, width), lambda i, s: (0, 0))] * 4
            + [
                pl.BlockSpec((4, tokens, width), lambda i, s: (0, 0, 0)),
                pl.BlockSpec((depth, 2 * columns), lambda i, s: (0, s[1])),
                pl.BlockSpec((depth, columns), lambda i, s: (0, 0)),
                pl.BlockSpec((depth, columns), lambda i, s: (0, 0)),
            ],
            out_specs=pl.BlockSpec((2, tokens // 2, 2 * columns), lambda i, s: (0, 0, 0)),
        ),
        compiler_params=pltpu.CompilerParams(vmem_limit_bytes=32 * 2**20),
        cost_estimate=pl.CostEstimate(
            flops=2 * tokens * 8 * width * 2 * columns, bytes_accessed=2**22, transcendentals=0
        ),
    )(place, *mine, other, out_weight, near_w, far_w)


def paired_plan(q_proj, k_proj, v_proj, filters, filter_blocks, out_weight):
    block, channels = q_proj.shape
    groups = filters.shape[0]
    g, z = lax.axis_index("group"), lax.axis_index("ctx")
    x, c = lax.axis_index("chan"), lax.axis_index("sub")
    pair, bit = z // 2, z % 2
    quarter = 2 * x + bit
    half, fourth = channels // 2, channels // 4
    place = jnp.stack([z, bit, quarter, (c == bit).astype(jnp.int32), pair, g]).astype(jnp.int32)

    def packed(quarter_index):
        k, v, q = (
            lax.dynamic_slice_in_dim(array, quarter_index * fourth, fourth, 1)
            for array in (k_proj, v_proj, q_proj)
        )
        product = (k.astype(jnp.float32) * v.astype(jnp.float32)).astype(jnp.bfloat16)
        return jnp.stack([product, q])

    tap_index = jnp.arange(filters.shape[1], dtype=jnp.int32)
    masked = jnp.where(tap_index[None, :] < filter_blocks[:, None] * block, filters, 0.0)
    masked = masked.astype(jnp.bfloat16)
    taken = groups // 4
    for_other = lax.dynamic_slice_in_dim(masked, (2 * (1 - x) + bit) * taken, taken, 0)
    filter_rows = for_other.reshape(-1, fourth)
    filter_rows = jnp.concatenate(
        [filter_rows, jnp.zeros((16 - filter_rows.shape[0], fourth), jnp.bfloat16)], axis=0
    )

    same_send = packed(2 * (1 - x) + bit)
    flip_send = jnp.concatenate(
        [packed(2 * (1 - x) + 1 - bit).reshape(2 * block, fourth), filter_rows], axis=0
    )
    same_came = swap(same_send, "chan")
    flip_came = swap(flip_send, "chan")
    same_own, flip_own = packed(2 * x + bit), packed(2 * x + 1 - bit)

    other_cols = (1 - bit) * half + g * fourth
    w_near = across(lax.dynamic_slice_in_dim(out_weight, other_cols, fourth, 1), 1)
    w_far = swap(w_near, "group")

    inside = pair == x
    piece_2 = across(jnp.where(inside, same_came, same_own), 2)
    piece_0 = jnp.where(inside, same_own, same_came)
    flip_came_pieces = flip_came[: 2 * block].reshape(2, block, fourth)
    piece_3 = across(jnp.where(inside, flip_came_pieces, flip_own), 3)
    piece_1 = across(jnp.where(inside, flip_own, flip_came_pieces), 1)

    taps = jnp.where(
        inside,
        lax.dynamic_slice_in_dim(masked, quarter * taken, taken, 0),
        flip_came[2 * block :].reshape(-1)[: taken * filters.shape[1]].reshape(taken, -1),
    ).astype(jnp.float32)
    first_rows = jnp.concatenate(
        [jnp.zeros((taken, 1), jnp.float32), taps[:, ::-1], jnp.zeros((taken, block - 1), jnp.float32)],
        axis=1,
    )
    first_rows, w_near, w_far = lax.optimization_barrier((first_rows, w_near, w_far))
    gated_far, gated_near = gated_conv(place, first_rows, (piece_0, piece_1, piece_2, piece_3))

    def partials(gated):
        mine = [gated, swap(gated, "ctx"), swap(gated, "chan"), swap(gated, "ctx", "chan")]
        other = swap(jnp.stack(mine), "sub")
        return project(place, mine, other, out_weight, w_near, w_far)

    far = partials(gated_far)
    far_own, far_near = across(far[0], 2), across(far[1], 3)
    close = partials(gated_near)
    near = across(close[1], 1)
    this_half = close[0].astype(jnp.float32) + far_own.astype(jnp.float32)
    that_half = near.astype(jnp.float32) + far_near.astype(jnp.float32)
    left = jnp.where(bit == 0, this_half, that_half)
    right = jnp.where(bit == 0, that_half, this_half)
    return jnp.concatenate([left, right], axis=1).astype(jnp.bfloat16)


def solution(mesh):
    sizes = dict(mesh.shape)

    def per_device(q_proj, k_proj, v_proj, filters, filter_blocks, out_weight):
        block, channels = q_proj.shape
        groups, taps = filters.shape
        paired = (
            (sizes["group"], sizes["ctx"], sizes["chan"], sizes["sub"]) == (2, 4, 2, 2)
            and taps == 2 * block
            and taps == channels // 2
            and groups % 4 == 0
            and (channels // groups) % 128 == 0
            and out_weight.shape == (channels, channels)
        )
        plan = paired_plan if paired else gathered_plan
        return plan(q_proj, k_proj, v_proj, filters, filter_blocks, out_weight)

    in_specs = (
        P(("group", "ctx"), ("chan", "sub")),
        P(("group", "ctx"), ("chan", "sub")),
        P(("group", "ctx"), ("chan", "sub")),
        P(("chan", "sub"), None),
        P(("chan", "sub")),
        P("ctx", ("chan", "sub")),
    )
    out_specs = P(("group", "ctx"), ("chan", "sub"))
    return jax.shard_map(
        per_device, mesh=mesh, in_specs=in_specs, out_specs=out_specs, check_vma=False
    )
```

```python
import math

import jax
import jax.numpy as jnp
from jax import lax
from jax.experimental import pallas as pl
from jax.experimental.pallas import tpu as pltpu
from jax.sharding import PartitionSpec as P


def shifted(value, axis, steps):
    count = lax.axis_size(axis)
    leading, last = (max(0, -steps), min(count, count - steps))
    return lax.ppermute(value, axis, [(source, source + steps) for source in range(leading, last)])


def forward_table(block_len, columns):
    length = 2 * block_len
    frequency = jnp.arange(block_len, dtype=jnp.int32)[:, None]
    positions = jnp.arange(columns, dtype=jnp.int32)[None, :]
    angles = (frequency * positions % length).astype(jnp.float32) * (2.0 * math.pi / length)
    alternating = (1 - 2 * (positions % 2)).astype(jnp.float32)
    upper = jnp.cos(angles)
    bottom = jnp.where(frequency == 0, alternating, -jnp.sin(angles))
    return jnp.concatenate([upper, bottom], axis=0)


def inverse_table(block_len):
    length = 2 * block_len
    samples = jnp.arange(block_len, dtype=jnp.int32)[:, None]
    frequency = jnp.arange(block_len, dtype=jnp.int32)[None, :]
    angles = (frequency * samples % length).astype(jnp.float32) * (2.0 * math.pi / length)
    alternating = (1 - 2 * (samples % 2)).astype(jnp.float32)
    left_half = jnp.where(frequency == 0, 1.0, 2.0 * jnp.cos(angles)) / length
    right_half = jnp.where(frequency == 0, alternating, -2.0 * jnp.sin(angles)) / length
    return jnp.concatenate([left_half, right_half], axis=1)


def packed_product(filter_spec, data_spec, first_row, block_len):
    filt_re = filter_spec[:block_len]
    filt_im = filter_spec[block_len:]
    data_re = data_spec[:block_len]
    data_im = data_spec[block_len:]
    other_rows = 1.0 - first_row
    upper = filt_re * data_re - filt_im * data_im * other_rows
    bottom = (filt_re * data_im + filt_im * data_re) * other_rows + filt_im * data_im * first_row
    return jnp.concatenate([upper, bottom], axis=0)


def gathered_plan(q_proj, k_proj, v_proj, filters, filter_blocks, out_weight):
    block_len, channels = q_proj.shape
    groups = filters.shape[0]
    per_group = channels // groups
    reach = lax.axis_size("ctx") // 2
    highest = lax.Precision.HIGHEST
    product = (k_proj.astype(jnp.float32) * v_proj.astype(jnp.float32)).astype(jnp.bfloat16)
    tap_index = jnp.arange(filters.shape[1], dtype=jnp.int32)
    masked = jnp.where(tap_index[None, :] < filter_blocks[:, None] * block_len, filters, 0.0)
    tap_blocks = masked.reshape(groups, reach, block_len)
    empty_block = jnp.zeros((groups, 1, block_len), jnp.float32)
    extended = jnp.concatenate([empty_block, tap_blocks, empty_block], axis=1)
    segments = jnp.concatenate([extended[:, 1:], extended[:, :-1]], axis=2)
    full_table = forward_table(block_len, 2 * block_len)
    filter_spectra = jnp.einsum("gdm,fm->dfg", segments, full_table, precision=highest)
    half_table = forward_table(block_len, block_len)
    table_high = half_table.astype(jnp.bfloat16)
    table_low = (half_table - table_high.astype(jnp.float32)).astype(jnp.bfloat16)
    first_row = (jnp.arange(block_len) == 0).astype(jnp.float32)[:, None, None]
    longest = jnp.max(filter_blocks)
    position = lax.axis_index("ctx")

    def transform(block):
        spectrum = jnp.dot(table_high, block, preferred_element_type=jnp.float32)
        spectrum = spectrum + jnp.dot(table_low, block, preferred_element_type=jnp.float32)
        return spectrum.reshape(2 * block_len, groups, per_group)

    def contribution(running, block, distance):
        filter_spec = lax.dynamic_index_in_dim(filter_spectra, distance, 0, keepdims=False)[
            :, :, None
        ]

        def add_term(partial_sum):
            return partial_sum + packed_product(filter_spec, transform(block), first_row, block_len)

        needed = (distance <= longest) & (position >= distance)
        return lax.cond(needed, add_term, lambda partial_sum: partial_sum, running)

    running = packed_product(
        filter_spectra[0][:, :, None], transform(product), first_row, block_len
    )

    def relay_step(distance, carry):
        carried, partial_sum = carry
        carried = shifted(carried, "ctx", 1)
        return (carried, contribution(partial_sum, carried, distance))

    carried, running = lax.fori_loop(1, reach + 1, relay_step, (product, running))
    spectrum_sum = running.reshape(2 * block_len, channels)
    conv = jnp.dot(inverse_table(block_len), spectrum_sum, precision=highest)
    gated = (q_proj.astype(jnp.float32) * conv).astype(jnp.bfloat16)
    all_gated = lax.all_gather(gated, ("chan", "sub"), axis=1, tiled=True)
    mixed = jnp.dot(
        all_gated,
        lax.all_gather(out_weight, "ctx", axis=0, tiled=True),
        preferred_element_type=jnp.float32,
    )
    return mixed.astype(jnp.bfloat16)


def swap(value, *axes):
    sizes = [lax.axis_size(axis) for axis in axes]
    total = math.prod(sizes)
    flip, stride = 0, 1
    for size in reversed(sizes):
        flip += stride
        stride *= size
    return lax.ppermute(value, axes, [(i, i ^ flip) for i in range(total)])


def across(value, distance):
    count = lax.axis_size("ctx")
    return lax.ppermute(value, "ctx", [(i, i ^ distance) for i in range(count)])


def gated_kernel(place, row_ref, *refs):
    pieces, outs, padded, gates = refs[:4], refs[4:6], refs[6], refs[7]
    _, block, width = pieces[0].shape
    groups, span = row_ref.shape
    per_group = width // groups
    padded[0] = jnp.zeros((block, width), padded.dtype)
    padded[1] = jnp.zeros((block, width), padded.dtype)
    for distance in range(4):
        token = place[0] ^ distance
        padded[2 + token] = pieces[distance][0]
        gates[token] = pieces[distance][1]
    for group in range(groups):
        columns = pl.ds(group * per_group, per_group)
        rows = jnp.broadcast_to(row_ref[group : group + 1, :], (block, span))
        toeplitz = pltpu.roll(rows, 0, 1, stride=1, stride_axis=0).astype(jnp.bfloat16)
        for out_ref, pair in zip(outs, (1 - place[4], place[4])):
            for part in range(2):
                token = 2 * pair + part
                source = jnp.concatenate(
                    [padded[token + step, :, columns] for step in range(3)], axis=0
                )
                conv = jnp.dot(toeplitz, source, preferred_element_type=jnp.float32)
                gated = gates[token, :, columns].astype(jnp.float32) * conv
                out_ref[pl.ds(part * block, block), columns] = gated.astype(out_ref.dtype)


def gated_conv(place, first_rows, pieces):
    _, block, width = pieces[0].shape
    return pl.pallas_call(
        gated_kernel,
        out_shape=[jax.ShapeDtypeStruct((2 * block, width), jnp.bfloat16)] * 2,
        grid_spec=pltpu.PrefetchScalarGridSpec(
            num_scalar_prefetch=1,
            grid=(1,),
            in_specs=[pl.BlockSpec(first_rows.shape, lambda i, s: (0, 0))]
            + [pl.BlockSpec((2, block, width), lambda i, s: (0, 0, 0))] * 4,
            out_specs=[pl.BlockSpec((2 * block, width), lambda i, s: (0, 0))] * 2,
            scratch_shapes=[
                pltpu.VMEM((6, block, width), jnp.bfloat16),
                pltpu.VMEM((4, block, width), jnp.bfloat16),
            ],
        ),
        compiler_params=pltpu.CompilerParams(vmem_limit_bytes=16 * 2**20),
        cost_estimate=pl.CostEstimate(
            flops=2 * 4 * block * 3 * block * width, bytes_accessed=2**21, transcendentals=0
        ),
    )(place, first_rows, *pieces)


def project_kernel(place, *refs):
    mine, other, own_w, near_w, far_w, out_ref = refs[:4], *refs[4:9]
    bit, quarter, same, group = place[1], place[2], place[3], place[5]
    tokens, width = mine[0].shape
    half = tokens // 2
    columns = near_w.shape[1]
    for part in range(2):
        rows = pl.ds(part * half, half)
        for got_w, index in ((near_w, group), (far_w, 1 - group)):
            place_of = pl.ds(pl.multiple_of(index * columns, columns), columns)
            total = jnp.zeros((half, columns), jnp.float32)
            for flip in range(4):
                here, there = mine[flip][rows, :], other[flip, rows, :]
                first = jnp.where(same == 1, here, there)
                second = jnp.where(same == 1, there, here)
                block = pl.ds(pl.multiple_of((quarter ^ flip) * width, width), width)
                total += jnp.dot(first, own_w[block, place_of], preferred_element_type=jnp.float32)
                total += jnp.dot(second, got_w[block, :], preferred_element_type=jnp.float32)
            out_ref[part ^ bit, :, place_of] = total.astype(out_ref.dtype)


def project(place, mine, other, out_weight, near_w, far_w):
    tokens, width = mine[0].shape
    depth, columns = near_w.shape
    return pl.pallas_call(
        project_kernel,
        out_shape=jax.ShapeDtypeStruct((2, tokens // 2, 2 * columns), jnp.bfloat16),
        grid_spec=pltpu.PrefetchScalarGridSpec(
            num_scalar_prefetch=1,
            grid=(1,),
            in_specs=[pl.BlockSpec((tokens, width), lambda i, s: (0, 0))] * 4
            + [
                pl.BlockSpec((4, tokens, width), lambda i, s: (0, 0, 0)),
                pl.BlockSpec((depth, 2 * columns), lambda i, s: (0, s[1])),
                pl.BlockSpec((depth, columns), lambda i, s: (0, 0)),
                pl.BlockSpec((depth, columns), lambda i, s: (0, 0)),
            ],
            out_specs=pl.BlockSpec((2, tokens // 2, 2 * columns), lambda i, s: (0, 0, 0)),
        ),
        compiler_params=pltpu.CompilerParams(vmem_limit_bytes=16 * 2**20),
        cost_estimate=pl.CostEstimate(
            flops=2 * tokens * 8 * width * 2 * columns, bytes_accessed=2**22, transcendentals=0
        ),
    )(place, *mine, other, out_weight, near_w, far_w)


def paired_plan(q_proj, k_proj, v_proj, filters, filter_blocks, out_weight):
    block, channels = q_proj.shape
    groups = filters.shape[0]
    g, z = lax.axis_index("group"), lax.axis_index("ctx")
    x, c = lax.axis_index("chan"), lax.axis_index("sub")
    pair, bit = z // 2, z % 2
    quarter = 2 * x + bit
    half, fourth = channels // 2, channels // 4
    place = jnp.stack([z, bit, quarter, (c == bit).astype(jnp.int32), pair, g]).astype(jnp.int32)

    def packed(quarter_index):
        k, v, q = (
            lax.dynamic_slice_in_dim(array, quarter_index * fourth, fourth, 1)
            for array in (k_proj, v_proj, q_proj)
        )
        product = (k.astype(jnp.float32) * v.astype(jnp.float32)).astype(jnp.bfloat16)
        return jnp.stack([product, q])

    tap_index = jnp.arange(filters.shape[1], dtype=jnp.int32)
    masked = jnp.where(tap_index[None, :] < filter_blocks[:, None] * block, filters, 0.0)
    masked = masked.astype(jnp.bfloat16)
    taken = groups // 4
    for_other = lax.dynamic_slice_in_dim(masked, (2 * (1 - x) + bit) * taken, taken, 0)
    filter_rows = for_other.reshape(-1, fourth)
    filter_rows = jnp.concatenate(
        [filter_rows, jnp.zeros((16 - filter_rows.shape[0], fourth), jnp.bfloat16)], axis=0
    )

    same_send = packed(2 * (1 - x) + bit)
    flip_send = jnp.concatenate(
        [packed(2 * (1 - x) + 1 - bit).reshape(2 * block, fourth), filter_rows], axis=0
    )
    same_came = swap(same_send, "chan")
    flip_came = swap(flip_send, "chan")
    same_own, flip_own = packed(2 * x + bit), packed(2 * x + 1 - bit)

    other_cols = (1 - bit) * half + g * fourth
    w_near = across(lax.dynamic_slice_in_dim(out_weight, other_cols, fourth, 1), 1)
    w_far = swap(w_near, "group")

    inside = pair == x
    piece_2 = across(jnp.where(inside, same_came, same_own), 2)
    piece_0 = jnp.where(inside, same_own, same_came)
    flip_came_pieces = flip_came[: 2 * block].reshape(2, block, fourth)
    piece_3 = across(jnp.where(inside, flip_came_pieces, flip_own), 3)
    piece_1 = across(jnp.where(inside, flip_own, flip_came_pieces), 1)

    taps = jnp.where(
        inside,
        lax.dynamic_slice_in_dim(masked, quarter * taken, taken, 0),
        flip_came[2 * block :].reshape(-1)[: taken * filters.shape[1]].reshape(taken, -1),
    ).astype(jnp.float32)
    first_rows = jnp.concatenate(
        [jnp.zeros((taken, 1), jnp.float32), taps[:, ::-1], jnp.zeros((taken, block - 1), jnp.float32)],
        axis=1,
    )
    first_rows, w_near, w_far = lax.optimization_barrier((first_rows, w_near, w_far))
    gated_far, gated_near = gated_conv(place, first_rows, (piece_0, piece_1, piece_2, piece_3))

    def gathered(gated):
        return [gated, swap(gated, "ctx"), swap(gated, "chan"), swap(gated, "ctx", "chan")]

    def partials(mine):
        return project(place, mine, swap(jnp.stack(mine), "sub"), out_weight, w_near, w_far)

    far = partials(gathered(gated_far))
    far_own, far_near = across(far[0], 2), across(far[1], 3)

    def close_partials(mine):
        gated, beside, cross = mine
        close = partials([gated, beside, cross, swap(beside, "chan")])
        return close[0], across(close[1], 1)

    def no_taps(mine):
        zeros = jnp.zeros((block, half), jnp.bfloat16)
        return zeros, zeros

    close_own, near = lax.cond(
        jnp.max(filter_blocks) > 0, close_partials, no_taps,
        [gated_near, swap(gated_near, "ctx"), swap(gated_near, "chan")],
    )
    this_half = close_own.astype(jnp.float32) + far_own.astype(jnp.float32)
    that_half = near.astype(jnp.float32) + far_near.astype(jnp.float32)
    left = jnp.where(bit == 0, this_half, that_half)
    right = jnp.where(bit == 0, that_half, this_half)
    return jnp.concatenate([left, right], axis=1).astype(jnp.bfloat16)


def solution(mesh):
    sizes = dict(mesh.shape)

    def per_device(q_proj, k_proj, v_proj, filters, filter_blocks, out_weight):
        block, channels = q_proj.shape
        groups, taps = filters.shape
        paired = (
            (sizes["group"], sizes["ctx"], sizes["chan"], sizes["sub"]) == (2, 4, 2, 2)
            and taps == 2 * block
            and taps == channels // 2
            and groups % 4 == 0
            and (channels // groups) % 128 == 0
            and out_weight.shape == (channels, channels)
        )
        plan = paired_plan if paired else gathered_plan
        return plan(q_proj, k_proj, v_proj, filters, filter_blocks, out_weight)

    in_specs = (
        P(("group", "ctx"), ("chan", "sub")),
        P(("group", "ctx"), ("chan", "sub")),
        P(("group", "ctx"), ("chan", "sub")),
        P(("chan", "sub"), None),
        P(("chan", "sub")),
        P("ctx", ("chan", "sub")),
    )
    out_specs = P(("group", "ctx"), ("chan", "sub"))
    return jax.shard_map(
        per_device, mesh=mesh, in_specs=in_specs, out_specs=out_specs, check_vma=False
    )
```

```python
import math

import jax
import jax.numpy as jnp
from jax import lax
from jax.experimental import pallas as pl
from jax.experimental.pallas import tpu as pltpu
from jax.sharding import PartitionSpec as P


def shifted(value, axis, steps):
    count = lax.axis_size(axis)
    leading, last = (max(0, -steps), min(count, count - steps))
    return lax.ppermute(value, axis, [(source, source + steps) for source in range(leading, last)])


def forward_table(block_len, columns):
    length = 2 * block_len
    frequency = jnp.arange(block_len, dtype=jnp.int32)[:, None]
    positions = jnp.arange(columns, dtype=jnp.int32)[None, :]
    angles = (frequency * positions % length).astype(jnp.float32) * (2.0 * math.pi / length)
    alternating = (1 - 2 * (positions % 2)).astype(jnp.float32)
    upper = jnp.cos(angles)
    bottom = jnp.where(frequency == 0, alternating, -jnp.sin(angles))
    return jnp.concatenate([upper, bottom], axis=0)


def inverse_table(block_len):
    length = 2 * block_len
    samples = jnp.arange(block_len, dtype=jnp.int32)[:, None]
    frequency = jnp.arange(block_len, dtype=jnp.int32)[None, :]
    angles = (frequency * samples % length).astype(jnp.float32) * (2.0 * math.pi / length)
    alternating = (1 - 2 * (samples % 2)).astype(jnp.float32)
    left_half = jnp.where(frequency == 0, 1.0, 2.0 * jnp.cos(angles)) / length
    right_half = jnp.where(frequency == 0, alternating, -2.0 * jnp.sin(angles)) / length
    return jnp.concatenate([left_half, right_half], axis=1)


def packed_product(filter_spec, data_spec, first_row, block_len):
    filt_re = filter_spec[:block_len]
    filt_im = filter_spec[block_len:]
    data_re = data_spec[:block_len]
    data_im = data_spec[block_len:]
    other_rows = 1.0 - first_row
    upper = filt_re * data_re - filt_im * data_im * other_rows
    bottom = (filt_re * data_im + filt_im * data_re) * other_rows + filt_im * data_im * first_row
    return jnp.concatenate([upper, bottom], axis=0)


def gathered_plan(q_proj, k_proj, v_proj, filters, filter_blocks, out_weight):
    block_len, channels = q_proj.shape
    groups = filters.shape[0]
    per_group = channels // groups
    reach = lax.axis_size("ctx") // 2
    highest = lax.Precision.HIGHEST
    product = (k_proj.astype(jnp.float32) * v_proj.astype(jnp.float32)).astype(jnp.bfloat16)
    tap_index = jnp.arange(filters.shape[1], dtype=jnp.int32)
    masked = jnp.where(tap_index[None, :] < filter_blocks[:, None] * block_len, filters, 0.0)
    tap_blocks = masked.reshape(groups, reach, block_len)
    empty_block = jnp.zeros((groups, 1, block_len), jnp.float32)
    extended = jnp.concatenate([empty_block, tap_blocks, empty_block], axis=1)
    segments = jnp.concatenate([extended[:, 1:], extended[:, :-1]], axis=2)
    full_table = forward_table(block_len, 2 * block_len)
    filter_spectra = jnp.einsum("gdm,fm->dfg", segments, full_table, precision=highest)
    half_table = forward_table(block_len, block_len)
    table_high = half_table.astype(jnp.bfloat16)
    table_low = (half_table - table_high.astype(jnp.float32)).astype(jnp.bfloat16)
    first_row = (jnp.arange(block_len) == 0).astype(jnp.float32)[:, None, None]
    longest = jnp.max(filter_blocks)
    position = lax.axis_index("ctx")

    def transform(block):
        spectrum = jnp.dot(table_high, block, preferred_element_type=jnp.float32)
        spectrum = spectrum + jnp.dot(table_low, block, preferred_element_type=jnp.float32)
        return spectrum.reshape(2 * block_len, groups, per_group)

    def contribution(running, block, distance):
        filter_spec = lax.dynamic_index_in_dim(filter_spectra, distance, 0, keepdims=False)[
            :, :, None
        ]

        def add_term(partial_sum):
            return partial_sum + packed_product(filter_spec, transform(block), first_row, block_len)

        needed = (distance <= longest) & (position >= distance)
        return lax.cond(needed, add_term, lambda partial_sum: partial_sum, running)

    running = packed_product(
        filter_spectra[0][:, :, None], transform(product), first_row, block_len
    )

    def relay_step(distance, carry):
        carried, partial_sum = carry
        carried = shifted(carried, "ctx", 1)
        return (carried, contribution(partial_sum, carried, distance))

    carried, running = lax.fori_loop(1, reach + 1, relay_step, (product, running))
    spectrum_sum = running.reshape(2 * block_len, channels)
    conv = jnp.dot(inverse_table(block_len), spectrum_sum, precision=highest)
    gated = (q_proj.astype(jnp.float32) * conv).astype(jnp.bfloat16)
    all_gated = lax.all_gather(gated, ("chan", "sub"), axis=1, tiled=True)
    mixed = jnp.dot(
        all_gated,
        lax.all_gather(out_weight, "ctx", axis=0, tiled=True),
        preferred_element_type=jnp.float32,
    )
    return mixed.astype(jnp.bfloat16)


def swap(value, *axes):
    sizes = [lax.axis_size(axis) for axis in axes]
    total = math.prod(sizes)
    flip, stride = 0, 1
    for size in reversed(sizes):
        flip += stride
        stride *= size
    return lax.ppermute(value, axes, [(i, i ^ flip) for i in range(total)])


def across(value, distance):
    count = lax.axis_size("ctx")
    return lax.ppermute(value, "ctx", [(i, i ^ distance) for i in range(count)])


VMEM = pl.BlockSpec(memory_space=pltpu.VMEM)


def local_call(kernel, out_shapes, *operands, scratch=(), flops=0):
    moved = sum(math.prod(o.shape) * o.dtype.itemsize for o in operands)
    return pl.pallas_call(
        kernel,
        out_shape=[jax.ShapeDtypeStruct(shape, jnp.bfloat16) for shape in out_shapes],
        in_specs=[VMEM] * len(operands),
        out_specs=[VMEM] * len(out_shapes),
        scratch_shapes=list(scratch),
        compiler_params=pltpu.CompilerParams(vmem_limit_bytes=16 * 2**20),
        cost_estimate=pl.CostEstimate(flops=flops, bytes_accessed=moved, transcendentals=0),
    )(*operands)


def where_am_i():
    z, x = lax.axis_index("ctx"), lax.axis_index("chan")
    pair, bit = z // 2, z % 2
    return z, x, pair, bit


def span(index, size):
    return pl.ds(pl.multiple_of(index * size, size), size)


def gated_kernel(place, row_ref, *refs):
    pieces, outs, padded, gates = refs[:4], refs[4:6], refs[6], refs[7]
    _, block, width = pieces[0].shape
    groups, span = row_ref.shape
    per_group = width // groups
    padded[0] = jnp.zeros((block, width), padded.dtype)
    padded[1] = jnp.zeros((block, width), padded.dtype)
    for distance in range(4):
        token = place[0] ^ distance
        padded[2 + token] = pieces[distance][0]
        gates[token] = pieces[distance][1]
    for group in range(groups):
        columns = pl.ds(group * per_group, per_group)
        rows = jnp.broadcast_to(row_ref[group : group + 1, :], (block, span))
        toeplitz = pltpu.roll(rows, 0, 1, stride=1, stride_axis=0).astype(jnp.bfloat16)
        for out_ref, pair in zip(outs, (1 - place[4], place[4])):
            for part in range(2):
                token = 2 * pair + part
                source = jnp.concatenate(
                    [padded[token + step, :, columns] for step in range(3)], axis=0
                )
                conv = jnp.dot(toeplitz, source, preferred_element_type=jnp.float32)
                gated = gates[token, :, columns].astype(jnp.float32) * conv
                out_ref[pl.ds(part * block, block), columns] = gated.astype(out_ref.dtype)


def gated_conv(place, first_rows, pieces):
    _, block, width = pieces[0].shape
    return pl.pallas_call(
        gated_kernel,
        out_shape=[jax.ShapeDtypeStruct((2 * block, width), jnp.bfloat16)] * 2,
        grid_spec=pltpu.PrefetchScalarGridSpec(
            num_scalar_prefetch=1,
            grid=(1,),
            in_specs=[pl.BlockSpec(first_rows.shape, lambda i, s: (0, 0))]
            + [pl.BlockSpec((2, block, width), lambda i, s: (0, 0, 0))] * 4,
            out_specs=[pl.BlockSpec((2 * block, width), lambda i, s: (0, 0))] * 2,
            scratch_shapes=[
                pltpu.VMEM((6, block, width), jnp.bfloat16),
                pltpu.VMEM((4, block, width), jnp.bfloat16),
            ],
        ),
        compiler_params=pltpu.CompilerParams(vmem_limit_bytes=16 * 2**20),
        cost_estimate=pl.CostEstimate(
            flops=2 * 4 * block * 3 * block * width, bytes_accessed=2**21, transcendentals=0
        ),
    )(place, first_rows, *pieces)


def project_kernel(place, *refs):
    mine, other, own_w, near_w, far_w, out_ref = refs[:4], *refs[4:9]
    bit, quarter, same, group = place[1], place[2], place[3], place[5]
    tokens, width = mine[0].shape
    half = tokens // 2
    columns = near_w.shape[1]
    for part in range(2):
        rows = pl.ds(part * half, half)
        for got_w, index in ((near_w, group), (far_w, 1 - group)):
            place_of = pl.ds(pl.multiple_of(index * columns, columns), columns)
            total = jnp.zeros((half, columns), jnp.float32)
            for flip in range(4):
                here, there = mine[flip][rows, :], other[flip, rows, :]
                first = jnp.where(same == 1, here, there)
                second = jnp.where(same == 1, there, here)
                block = pl.ds(pl.multiple_of((quarter ^ flip) * width, width), width)
                total += jnp.dot(first, own_w[block, place_of], preferred_element_type=jnp.float32)
                total += jnp.dot(second, got_w[block, :], preferred_element_type=jnp.float32)
            out_ref[part ^ bit, :, place_of] = total.astype(out_ref.dtype)


def project(place, mine, other, out_weight, near_w, far_w):
    tokens, width = mine[0].shape
    depth, columns = near_w.shape
    return pl.pallas_call(
        project_kernel,
        out_shape=jax.ShapeDtypeStruct((2, tokens // 2, 2 * columns), jnp.bfloat16),
        grid_spec=pltpu.PrefetchScalarGridSpec(
            num_scalar_prefetch=1,
            grid=(1,),
            in_specs=[pl.BlockSpec((tokens, width), lambda i, s: (0, 0))] * 4
            + [
                pl.BlockSpec((4, tokens, width), lambda i, s: (0, 0, 0)),
                pl.BlockSpec((depth, 2 * columns), lambda i, s: (0, s[1])),
                pl.BlockSpec((depth, columns), lambda i, s: (0, 0)),
                pl.BlockSpec((depth, columns), lambda i, s: (0, 0)),
            ],
            out_specs=pl.BlockSpec((2, tokens // 2, 2 * columns), lambda i, s: (0, 0, 0)),
        ),
        compiler_params=pltpu.CompilerParams(vmem_limit_bytes=16 * 2**20),
        cost_estimate=pl.CostEstimate(
            flops=2 * tokens * 8 * width * 2 * columns, bytes_accessed=2**22, transcendentals=0
        ),
    )(place, *mine, other, out_weight, near_w, far_w)


def project_whole_kernel(*refs):
    mine, other, own_w, near_w, far_w, outs = refs[:4], *refs[4:8], refs[8:10]
    _, x, _, bit = where_am_i()
    group, same = lax.axis_index("group"), lax.axis_index("sub") == bit
    tokens, width = mine[0].shape
    half = tokens // 2
    columns = near_w.shape[1]
    for slot in range(2):
        rows = span(slot ^ bit, half)
        for got_w, index in ((near_w, group), (far_w, 1 - group)):
            total = jnp.zeros((half, columns), jnp.float32)
            for flip in range(4):
                here, there = mine[flip][rows, :], other[flip, rows, :]
                first = jnp.where(same, here, there)
                second = jnp.where(same, there, here)
                block = span((2 * x + bit) ^ flip, width)
                own_part = own_w[block, span(2 * bit + index, columns)]
                total += jnp.dot(first, own_part, preferred_element_type=jnp.float32)
                total += jnp.dot(second, got_w[block, :], preferred_element_type=jnp.float32)
            outs[slot][:, span(index, columns)] = total.astype(outs[slot].dtype)


def paired_plan(q_proj, k_proj, v_proj, filters, filter_blocks, out_weight):
    block, channels = q_proj.shape
    groups = filters.shape[0]
    g, z = lax.axis_index("group"), lax.axis_index("ctx")
    x, c = lax.axis_index("chan"), lax.axis_index("sub")
    pair, bit = z // 2, z % 2
    quarter = 2 * x + bit
    half, fourth = channels // 2, channels // 4
    place = jnp.stack([z, bit, quarter, (c == bit).astype(jnp.int32), pair, g]).astype(jnp.int32)

    def packed(quarter_index):
        k, v, q = (
            lax.dynamic_slice_in_dim(array, quarter_index * fourth, fourth, 1)
            for array in (k_proj, v_proj, q_proj)
        )
        product = (k.astype(jnp.float32) * v.astype(jnp.float32)).astype(jnp.bfloat16)
        return jnp.stack([product, q])

    tap_index = jnp.arange(filters.shape[1], dtype=jnp.int32)
    masked = jnp.where(tap_index[None, :] < filter_blocks[:, None] * block, filters, 0.0)
    masked = masked.astype(jnp.bfloat16)
    taken = groups // 4
    for_other = lax.dynamic_slice_in_dim(masked, (2 * (1 - x) + bit) * taken, taken, 0)
    filter_rows = for_other.reshape(-1, fourth)
    filter_rows = jnp.concatenate(
        [filter_rows, jnp.zeros((16 - filter_rows.shape[0], fourth), jnp.bfloat16)], axis=0
    )

    same_send = packed(2 * (1 - x) + bit)
    flip_send = jnp.concatenate(
        [packed(2 * (1 - x) + 1 - bit).reshape(2 * block, fourth), filter_rows], axis=0
    )
    same_came = swap(same_send, "chan")
    flip_came = swap(flip_send, "chan")
    same_own, flip_own = packed(2 * x + bit), packed(2 * x + 1 - bit)

    other_cols = (1 - bit) * half + g * fourth
    w_near = across(lax.dynamic_slice_in_dim(out_weight, other_cols, fourth, 1), 1)
    w_far = swap(w_near, "group")

    inside = pair == x
    piece_2 = across(jnp.where(inside, same_came, same_own), 2)
    piece_0 = jnp.where(inside, same_own, same_came)
    flip_came_pieces = flip_came[: 2 * block].reshape(2, block, fourth)
    piece_3 = across(jnp.where(inside, flip_came_pieces, flip_own), 3)
    piece_1 = across(jnp.where(inside, flip_own, flip_came_pieces), 1)

    taps = jnp.where(
        inside,
        lax.dynamic_slice_in_dim(masked, quarter * taken, taken, 0),
        flip_came[2 * block :].reshape(-1)[: taken * filters.shape[1]].reshape(taken, -1),
    ).astype(jnp.float32)
    first_rows = jnp.concatenate(
        [jnp.zeros((taken, 1), jnp.float32), taps[:, ::-1], jnp.zeros((taken, block - 1), jnp.float32)],
        axis=1,
    )
    first_rows, w_near, w_far = lax.optimization_barrier((first_rows, w_near, w_far))
    gated_far, gated_near = gated_conv(place, first_rows, (piece_0, piece_1, piece_2, piece_3))

    def gathered(gated):
        return [gated, swap(gated, "ctx"), swap(gated, "chan"), swap(gated, "ctx", "chan")]

    def partials(mine):
        other = swap(jnp.stack(mine), "sub")
        return local_call(
            project_whole_kernel, [(block, half)] * 2, *mine, other, out_weight, w_near, w_far,
            flops=8 * block * channels * half // 2,
        )

    far = partials(gathered(gated_far))
    far_own, far_near = across(far[0], 2), across(far[1], 3)

    def close_partials(mine):
        gated, beside, cross = mine
        close = partials([gated, beside, cross, swap(beside, "chan")])
        return close[0], across(close[1], 1)

    def no_taps(mine):
        zeros = jnp.zeros((block, half), jnp.bfloat16)
        return zeros, zeros

    close_own, near = lax.cond(
        jnp.max(filter_blocks) > 0, close_partials, no_taps,
        [gated_near, swap(gated_near, "ctx"), swap(gated_near, "chan")],
    )
    this_half = close_own.astype(jnp.float32) + far_own.astype(jnp.float32)
    that_half = near.astype(jnp.float32) + far_near.astype(jnp.float32)
    left = jnp.where(bit == 0, this_half, that_half)
    right = jnp.where(bit == 0, that_half, this_half)
    return jnp.concatenate([left, right], axis=1).astype(jnp.bfloat16)


def solution(mesh):
    sizes = dict(mesh.shape)

    def per_device(q_proj, k_proj, v_proj, filters, filter_blocks, out_weight):
        block, channels = q_proj.shape
        groups, taps = filters.shape
        paired = (
            (sizes["group"], sizes["ctx"], sizes["chan"], sizes["sub"]) == (2, 4, 2, 2)
            and taps == 2 * block
            and taps == channels // 2
            and groups % 4 == 0
            and (channels // groups) % 128 == 0
            and out_weight.shape == (channels, channels)
        )
        plan = paired_plan if paired else gathered_plan
        return plan(q_proj, k_proj, v_proj, filters, filter_blocks, out_weight)

    in_specs = (
        P(("group", "ctx"), ("chan", "sub")),
        P(("group", "ctx"), ("chan", "sub")),
        P(("group", "ctx"), ("chan", "sub")),
        P(("chan", "sub"), None),
        P(("chan", "sub")),
        P("ctx", ("chan", "sub")),
    )
    out_specs = P(("group", "ctx"), ("chan", "sub"))
    return jax.shard_map(
        per_device, mesh=mesh, in_specs=in_specs, out_specs=out_specs, check_vma=False
    )
```

```python
import math

import jax
import jax.numpy as jnp
from jax import lax
from jax.experimental import pallas as pl
from jax.experimental.pallas import tpu as pltpu
from jax.sharding import PartitionSpec as P


def shifted(value, axis, steps):
    count = lax.axis_size(axis)
    leading, last = (max(0, -steps), min(count, count - steps))
    return lax.ppermute(value, axis, [(source, source + steps) for source in range(leading, last)])


def forward_table(block_len, columns):
    length = 2 * block_len
    frequency = jnp.arange(block_len, dtype=jnp.int32)[:, None]
    positions = jnp.arange(columns, dtype=jnp.int32)[None, :]
    angles = (frequency * positions % length).astype(jnp.float32) * (2.0 * math.pi / length)
    alternating = (1 - 2 * (positions % 2)).astype(jnp.float32)
    upper = jnp.cos(angles)
    bottom = jnp.where(frequency == 0, alternating, -jnp.sin(angles))
    return jnp.concatenate([upper, bottom], axis=0)


def inverse_table(block_len):
    length = 2 * block_len
    samples = jnp.arange(block_len, dtype=jnp.int32)[:, None]
    frequency = jnp.arange(block_len, dtype=jnp.int32)[None, :]
    angles = (frequency * samples % length).astype(jnp.float32) * (2.0 * math.pi / length)
    alternating = (1 - 2 * (samples % 2)).astype(jnp.float32)
    left_half = jnp.where(frequency == 0, 1.0, 2.0 * jnp.cos(angles)) / length
    right_half = jnp.where(frequency == 0, alternating, -2.0 * jnp.sin(angles)) / length
    return jnp.concatenate([left_half, right_half], axis=1)


def packed_product(filter_spec, data_spec, first_row, block_len):
    filt_re = filter_spec[:block_len]
    filt_im = filter_spec[block_len:]
    data_re = data_spec[:block_len]
    data_im = data_spec[block_len:]
    other_rows = 1.0 - first_row
    upper = filt_re * data_re - filt_im * data_im * other_rows
    bottom = (filt_re * data_im + filt_im * data_re) * other_rows + filt_im * data_im * first_row
    return jnp.concatenate([upper, bottom], axis=0)


def gathered_plan(q_proj, k_proj, v_proj, filters, filter_blocks, out_weight):
    block_len, channels = q_proj.shape
    groups = filters.shape[0]
    per_group = channels // groups
    reach = lax.axis_size("ctx") // 2
    highest = lax.Precision.HIGHEST
    product = (k_proj.astype(jnp.float32) * v_proj.astype(jnp.float32)).astype(jnp.bfloat16)
    tap_index = jnp.arange(filters.shape[1], dtype=jnp.int32)
    masked = jnp.where(tap_index[None, :] < filter_blocks[:, None] * block_len, filters, 0.0)
    tap_blocks = masked.reshape(groups, reach, block_len)
    empty_block = jnp.zeros((groups, 1, block_len), jnp.float32)
    extended = jnp.concatenate([empty_block, tap_blocks, empty_block], axis=1)
    segments = jnp.concatenate([extended[:, 1:], extended[:, :-1]], axis=2)
    full_table = forward_table(block_len, 2 * block_len)
    filter_spectra = jnp.einsum("gdm,fm->dfg", segments, full_table, precision=highest)
    half_table = forward_table(block_len, block_len)
    table_high = half_table.astype(jnp.bfloat16)
    table_low = (half_table - table_high.astype(jnp.float32)).astype(jnp.bfloat16)
    first_row = (jnp.arange(block_len) == 0).astype(jnp.float32)[:, None, None]
    longest = jnp.max(filter_blocks)
    position = lax.axis_index("ctx")

    def transform(block):
        spectrum = jnp.dot(table_high, block, preferred_element_type=jnp.float32)
        spectrum = spectrum + jnp.dot(table_low, block, preferred_element_type=jnp.float32)
        return spectrum.reshape(2 * block_len, groups, per_group)

    def contribution(running, block, distance):
        filter_spec = lax.dynamic_index_in_dim(filter_spectra, distance, 0, keepdims=False)[
            :, :, None
        ]

        def add_term(partial_sum):
            return partial_sum + packed_product(filter_spec, transform(block), first_row, block_len)

        needed = (distance <= longest) & (position >= distance)
        return lax.cond(needed, add_term, lambda partial_sum: partial_sum, running)

    running = packed_product(
        filter_spectra[0][:, :, None], transform(product), first_row, block_len
    )

    def relay_step(distance, carry):
        carried, partial_sum = carry
        carried = shifted(carried, "ctx", 1)
        return (carried, contribution(partial_sum, carried, distance))

    carried, running = lax.fori_loop(1, reach + 1, relay_step, (product, running))
    spectrum_sum = running.reshape(2 * block_len, channels)
    conv = jnp.dot(inverse_table(block_len), spectrum_sum, precision=highest)
    gated = (q_proj.astype(jnp.float32) * conv).astype(jnp.bfloat16)
    all_gated = lax.all_gather(gated, ("chan", "sub"), axis=1, tiled=True)
    mixed = jnp.dot(
        all_gated,
        lax.all_gather(out_weight, "ctx", axis=0, tiled=True),
        preferred_element_type=jnp.float32,
    )
    return mixed.astype(jnp.bfloat16)


def swap(value, *axes):
    sizes = [lax.axis_size(axis) for axis in axes]
    total = math.prod(sizes)
    flip, stride = 0, 1
    for size in reversed(sizes):
        flip += stride
        stride *= size
    return lax.ppermute(value, axes, [(i, i ^ flip) for i in range(total)])


def across(value, distance):
    count = lax.axis_size("ctx")
    return lax.ppermute(value, "ctx", [(i, i ^ distance) for i in range(count)])


VMEM = pl.BlockSpec(memory_space=pltpu.VMEM)


def local_call(kernel, out_shapes, *operands, scratch=(), flops=0):
    moved = sum(math.prod(o.shape) * o.dtype.itemsize for o in operands)
    return pl.pallas_call(
        kernel,
        out_shape=[jax.ShapeDtypeStruct(shape, jnp.bfloat16) for shape in out_shapes],
        in_specs=[VMEM] * len(operands),
        out_specs=[VMEM] * len(out_shapes),
        scratch_shapes=list(scratch),
        compiler_params=pltpu.CompilerParams(vmem_limit_bytes=16 * 2**20),
        cost_estimate=pl.CostEstimate(flops=flops, bytes_accessed=moved, transcendentals=0),
    )(*operands)


def where_am_i():
    z, x = lax.axis_index("ctx"), lax.axis_index("chan")
    pair, bit = z // 2, z % 2
    return z, x, pair, bit


def span(index, size):
    return pl.ds(pl.multiple_of(index * size, size), size)


def gated_kernel(place, row_ref, *refs):
    pieces, outs, padded, gates = refs[:4], refs[4:6], refs[6], refs[7]
    _, block, width = pieces[0].shape
    groups, span = row_ref.shape
    per_group = width // groups
    padded[0] = jnp.zeros((block, width), padded.dtype)
    padded[1] = jnp.zeros((block, width), padded.dtype)
    for distance in range(4):
        token = place[0] ^ distance
        padded[2 + token] = pieces[distance][0]
        gates[token] = pieces[distance][1]
    for group in range(groups):
        columns = pl.ds(group * per_group, per_group)
        rows = jnp.broadcast_to(row_ref[group : group + 1, :], (block, span))
        toeplitz = pltpu.roll(rows, 0, 1, stride=1, stride_axis=0).astype(jnp.bfloat16)
        for out_ref, pair in zip(outs, (1 - place[4], place[4])):
            for part in range(2):
                token = 2 * pair + part
                source = jnp.concatenate(
                    [padded[token + step, :, columns] for step in range(3)], axis=0
                )
                conv = jnp.dot(toeplitz, source, preferred_element_type=jnp.float32)
                gated = gates[token, :, columns].astype(jnp.float32) * conv
                out_ref[pl.ds(part * block, block), columns] = gated.astype(out_ref.dtype)


def gated_conv(place, first_rows, pieces):
    _, block, width = pieces[0].shape
    return pl.pallas_call(
        gated_kernel,
        out_shape=[jax.ShapeDtypeStruct((2 * block, width), jnp.bfloat16)] * 2,
        grid_spec=pltpu.PrefetchScalarGridSpec(
            num_scalar_prefetch=1,
            grid=(1,),
            in_specs=[pl.BlockSpec(first_rows.shape, lambda i, s: (0, 0))]
            + [pl.BlockSpec((2, block, width), lambda i, s: (0, 0, 0))] * 4,
            out_specs=[pl.BlockSpec((2 * block, width), lambda i, s: (0, 0))] * 2,
            scratch_shapes=[
                pltpu.VMEM((6, block, width), jnp.bfloat16),
                pltpu.VMEM((4, block, width), jnp.bfloat16),
            ],
        ),
        compiler_params=pltpu.CompilerParams(vmem_limit_bytes=16 * 2**20),
        cost_estimate=pl.CostEstimate(
            flops=2 * 4 * block * 3 * block * width, bytes_accessed=2**21, transcendentals=0
        ),
    )(place, first_rows, *pieces)


def project_kernel(place, *refs):
    mine, other, own_w, near_w, far_w, out_ref = refs[:4], *refs[4:9]
    bit, quarter, same, group = place[1], place[2], place[3], place[5]
    tokens, width = mine[0].shape
    half = tokens // 2
    columns = near_w.shape[1]
    for part in range(2):
        rows = pl.ds(part * half, half)
        for got_w, index in ((near_w, group), (far_w, 1 - group)):
            place_of = pl.ds(pl.multiple_of(index * columns, columns), columns)
            total = jnp.zeros((half, columns), jnp.float32)
            for flip in range(4):
                here, there = mine[flip][rows, :], other[flip, rows, :]
                first = jnp.where(same == 1, here, there)
                second = jnp.where(same == 1, there, here)
                block = pl.ds(pl.multiple_of((quarter ^ flip) * width, width), width)
                total += jnp.dot(first, own_w[block, place_of], preferred_element_type=jnp.float32)
                total += jnp.dot(second, got_w[block, :], preferred_element_type=jnp.float32)
            out_ref[part ^ bit, :, place_of] = total.astype(out_ref.dtype)


def project(place, mine, other, out_weight, near_w, far_w):
    tokens, width = mine[0].shape
    depth, columns = near_w.shape
    return pl.pallas_call(
        project_kernel,
        out_shape=jax.ShapeDtypeStruct((2, tokens // 2, 2 * columns), jnp.bfloat16),
        grid_spec=pltpu.PrefetchScalarGridSpec(
            num_scalar_prefetch=1,
            grid=(1,),
            in_specs=[pl.BlockSpec((tokens, width), lambda i, s: (0, 0))] * 4
            + [
                pl.BlockSpec((4, tokens, width), lambda i, s: (0, 0, 0)),
                pl.BlockSpec((depth, 2 * columns), lambda i, s: (0, s[1])),
                pl.BlockSpec((depth, columns), lambda i, s: (0, 0)),
                pl.BlockSpec((depth, columns), lambda i, s: (0, 0)),
            ],
            out_specs=pl.BlockSpec((2, tokens // 2, 2 * columns), lambda i, s: (0, 0, 0)),
        ),
        compiler_params=pltpu.CompilerParams(vmem_limit_bytes=16 * 2**20),
        cost_estimate=pl.CostEstimate(
            flops=2 * tokens * 8 * width * 2 * columns, bytes_accessed=2**22, transcendentals=0
        ),
    )(place, *mine, other, out_weight, near_w, far_w)


def project_whole_kernel(*refs):
    mine, other, own_w, near_w, far_w, outs = refs[:4], *refs[4:8], refs[8:10]
    _, x, _, bit = where_am_i()
    group, same = lax.axis_index("group"), lax.axis_index("sub") == bit
    tokens, width = mine[0].shape
    half = tokens // 2
    columns = near_w.shape[1]
    blocks = [span((2 * x + bit) ^ flip, width) for flip in range(4)]

    def fill(first, second):
        for got_w, index in ((near_w, group), (far_w, 1 - group)):
            place = span(2 * bit + index, columns)
            own_part = jnp.concatenate([own_w[block, place] for block in blocks], axis=0)
            got_part = jnp.concatenate([got_w[block, :] for block in blocks], axis=0)
            for slot in range(2):
                rows = span(slot ^ bit, half)
                total = jnp.dot(
                    jnp.concatenate([ref[rows, :] for ref in first], axis=1),
                    own_part,
                    preferred_element_type=jnp.float32,
                )
                total += jnp.dot(
                    jnp.concatenate([ref[rows, :] for ref in second], axis=1),
                    got_part,
                    preferred_element_type=jnp.float32,
                )
                outs[slot][:, span(index, columns)] = total.astype(outs[slot].dtype)

    others = [other.at[flip] for flip in range(4)]

    @pl.when(same)
    def _():
        fill(mine, others)

    @pl.when(jnp.logical_not(same))
    def _():
        fill(others, mine)


def paired_plan(q_proj, k_proj, v_proj, filters, filter_blocks, out_weight):
    block, channels = q_proj.shape
    groups = filters.shape[0]
    g, z = lax.axis_index("group"), lax.axis_index("ctx")
    x, c = lax.axis_index("chan"), lax.axis_index("sub")
    pair, bit = z // 2, z % 2
    quarter = 2 * x + bit
    half, fourth = channels // 2, channels // 4
    place = jnp.stack([z, bit, quarter, (c == bit).astype(jnp.int32), pair, g]).astype(jnp.int32)

    def packed(quarter_index):
        k, v, q = (
            lax.dynamic_slice_in_dim(array, quarter_index * fourth, fourth, 1)
            for array in (k_proj, v_proj, q_proj)
        )
        product = (k.astype(jnp.float32) * v.astype(jnp.float32)).astype(jnp.bfloat16)
        return jnp.stack([product, q])

    tap_index = jnp.arange(filters.shape[1], dtype=jnp.int32)
    masked = jnp.where(tap_index[None, :] < filter_blocks[:, None] * block, filters, 0.0)
    masked = masked.astype(jnp.bfloat16)
    taken = groups // 4
    for_other = lax.dynamic_slice_in_dim(masked, (2 * (1 - x) + bit) * taken, taken, 0)
    filter_rows = for_other.reshape(-1, fourth)
    filter_rows = jnp.concatenate(
        [filter_rows, jnp.zeros((16 - filter_rows.shape[0], fourth), jnp.bfloat16)], axis=0
    )

    same_send = packed(2 * (1 - x) + bit)
    k_proj, v_proj, q_proj, same_send = lax.optimization_barrier((k_proj, v_proj, q_proj, same_send))
    flip_send = jnp.concatenate(
        [packed(2 * (1 - x) + 1 - bit).reshape(2 * block, fourth), filter_rows], axis=0
    )
    same_came = swap(same_send, "chan")
    flip_came = swap(flip_send, "chan")
    same_own, flip_own = packed(2 * x + bit), packed(2 * x + 1 - bit)

    other_cols = (1 - bit) * half + g * fourth
    w_near = across(lax.dynamic_slice_in_dim(out_weight, other_cols, fourth, 1), 1)
    w_far = swap(w_near, "group")

    inside = pair == x
    piece_2 = across(jnp.where(inside, same_came, same_own), 2)
    piece_0 = jnp.where(inside, same_own, same_came)
    flip_came_pieces = flip_came[: 2 * block].reshape(2, block, fourth)
    piece_3 = across(jnp.where(inside, flip_came_pieces, flip_own), 3)
    piece_1 = across(jnp.where(inside, flip_own, flip_came_pieces), 1)

    taps = jnp.where(
        inside,
        lax.dynamic_slice_in_dim(masked, quarter * taken, taken, 0),
        flip_came[2 * block :].reshape(-1)[: taken * filters.shape[1]].reshape(taken, -1),
    ).astype(jnp.float32)
    first_rows = jnp.concatenate(
        [jnp.zeros((taken, 1), jnp.float32), taps[:, ::-1], jnp.zeros((taken, block - 1), jnp.float32)],
        axis=1,
    )
    first_rows, w_near, w_far = lax.optimization_barrier((first_rows, w_near, w_far))
    gated_far, gated_near = gated_conv(place, first_rows, (piece_0, piece_1, piece_2, piece_3))

    def gathered(gated):
        return [gated, swap(gated, "ctx"), swap(gated, "chan"), swap(gated, "ctx", "chan")]

    def partials(mine):
        other = swap(jnp.stack(mine), "sub")
        return local_call(
            project_whole_kernel, [(block, half)] * 2, *mine, other, out_weight, w_near, w_far,
            flops=8 * block * channels * half // 2,
        )

    far = partials(gathered(gated_far))
    far_own, far_near = across(far[0], 2), across(far[1], 3)

    def close_partials(mine):
        gated, beside, cross = mine
        close = partials([gated, beside, cross, swap(beside, "chan")])
        return close[0], across(close[1], 1)

    def no_taps(mine):
        zeros = jnp.zeros((block, half), jnp.bfloat16)
        return zeros, zeros

    close_own, near = lax.cond(
        jnp.max(filter_blocks) > 0, close_partials, no_taps,
        [gated_near, swap(gated_near, "ctx"), swap(gated_near, "chan")],
    )
    this_half = close_own.astype(jnp.float32) + far_own.astype(jnp.float32)
    that_half = near.astype(jnp.float32) + far_near.astype(jnp.float32)
    left = jnp.where(bit == 0, this_half, that_half)
    right = jnp.where(bit == 0, that_half, this_half)
    return jnp.concatenate([left, right], axis=1).astype(jnp.bfloat16)


def solution(mesh):
    sizes = dict(mesh.shape)

    def per_device(q_proj, k_proj, v_proj, filters, filter_blocks, out_weight):
        block, channels = q_proj.shape
        groups, taps = filters.shape
        paired = (
            (sizes["group"], sizes["ctx"], sizes["chan"], sizes["sub"]) == (2, 4, 2, 2)
            and taps == 2 * block
            and taps == channels // 2
            and groups % 4 == 0
            and (channels // groups) % 128 == 0
            and out_weight.shape == (channels, channels)
        )
        plan = paired_plan if paired else gathered_plan
        return plan(q_proj, k_proj, v_proj, filters, filter_blocks, out_weight)

    in_specs = (
        P(("group", "ctx"), ("chan", "sub")),
        P(("group", "ctx"), ("chan", "sub")),
        P(("group", "ctx"), ("chan", "sub")),
        P(("chan", "sub"), None),
        P(("chan", "sub")),
        P("ctx", ("chan", "sub")),
    )
    out_specs = P(("group", "ctx"), ("chan", "sub"))
    return jax.shard_map(
        per_device, mesh=mesh, in_specs=in_specs, out_specs=out_specs, check_vma=False
    )
```

```python
import functools
import math

import jax
import jax.numpy as jnp
from jax import lax
from jax.experimental import pallas as pl
from jax.experimental.pallas import tpu as pltpu
from jax.sharding import PartitionSpec as P


def shifted(value, axis, steps):
    count = lax.axis_size(axis)
    leading, last = (max(0, -steps), min(count, count - steps))
    return lax.ppermute(value, axis, [(source, source + steps) for source in range(leading, last)])


def forward_table(block_len, columns):
    length = 2 * block_len
    frequency = jnp.arange(block_len, dtype=jnp.int32)[:, None]
    positions = jnp.arange(columns, dtype=jnp.int32)[None, :]
    angles = (frequency * positions % length).astype(jnp.float32) * (2.0 * math.pi / length)
    alternating = (1 - 2 * (positions % 2)).astype(jnp.float32)
    upper = jnp.cos(angles)
    bottom = jnp.where(frequency == 0, alternating, -jnp.sin(angles))
    return jnp.concatenate([upper, bottom], axis=0)


def inverse_table(block_len):
    length = 2 * block_len
    samples = jnp.arange(block_len, dtype=jnp.int32)[:, None]
    frequency = jnp.arange(block_len, dtype=jnp.int32)[None, :]
    angles = (frequency * samples % length).astype(jnp.float32) * (2.0 * math.pi / length)
    alternating = (1 - 2 * (samples % 2)).astype(jnp.float32)
    left_half = jnp.where(frequency == 0, 1.0, 2.0 * jnp.cos(angles)) / length
    right_half = jnp.where(frequency == 0, alternating, -2.0 * jnp.sin(angles)) / length
    return jnp.concatenate([left_half, right_half], axis=1)


def packed_product(filter_spec, data_spec, first_row, block_len):
    filt_re = filter_spec[:block_len]
    filt_im = filter_spec[block_len:]
    data_re = data_spec[:block_len]
    data_im = data_spec[block_len:]
    other_rows = 1.0 - first_row
    upper = filt_re * data_re - filt_im * data_im * other_rows
    bottom = (filt_re * data_im + filt_im * data_re) * other_rows + filt_im * data_im * first_row
    return jnp.concatenate([upper, bottom], axis=0)


def gathered_plan(q_proj, k_proj, v_proj, filters, filter_blocks, out_weight):
    block_len, channels = q_proj.shape
    groups = filters.shape[0]
    per_group = channels // groups
    reach = lax.axis_size("ctx") // 2
    highest = lax.Precision.HIGHEST
    product = (k_proj.astype(jnp.float32) * v_proj.astype(jnp.float32)).astype(jnp.bfloat16)
    tap_index = jnp.arange(filters.shape[1], dtype=jnp.int32)
    masked = jnp.where(tap_index[None, :] < filter_blocks[:, None] * block_len, filters, 0.0)
    tap_blocks = masked.reshape(groups, reach, block_len)
    empty_block = jnp.zeros((groups, 1, block_len), jnp.float32)
    extended = jnp.concatenate([empty_block, tap_blocks, empty_block], axis=1)
    segments = jnp.concatenate([extended[:, 1:], extended[:, :-1]], axis=2)
    full_table = forward_table(block_len, 2 * block_len)
    filter_spectra = jnp.einsum("gdm,fm->dfg", segments, full_table, precision=highest)
    half_table = forward_table(block_len, block_len)
    table_high = half_table.astype(jnp.bfloat16)
    table_low = (half_table - table_high.astype(jnp.float32)).astype(jnp.bfloat16)
    first_row = (jnp.arange(block_len) == 0).astype(jnp.float32)[:, None, None]
    longest = jnp.max(filter_blocks)
    position = lax.axis_index("ctx")

    def transform(block):
        spectrum = jnp.dot(table_high, block, preferred_element_type=jnp.float32)
        spectrum = spectrum + jnp.dot(table_low, block, preferred_element_type=jnp.float32)
        return spectrum.reshape(2 * block_len, groups, per_group)

    def contribution(running, block, distance):
        filter_spec = lax.dynamic_index_in_dim(filter_spectra, distance, 0, keepdims=False)[
            :, :, None
        ]

        def add_term(partial_sum):
            return partial_sum + packed_product(filter_spec, transform(block), first_row, block_len)

        needed = (distance <= longest) & (position >= distance)
        return lax.cond(needed, add_term, lambda partial_sum: partial_sum, running)

    running = packed_product(
        filter_spectra[0][:, :, None], transform(product), first_row, block_len
    )

    def relay_step(distance, carry):
        carried, partial_sum = carry
        carried = shifted(carried, "ctx", 1)
        return (carried, contribution(partial_sum, carried, distance))

    carried, running = lax.fori_loop(1, reach + 1, relay_step, (product, running))
    spectrum_sum = running.reshape(2 * block_len, channels)
    conv = jnp.dot(inverse_table(block_len), spectrum_sum, precision=highest)
    gated = (q_proj.astype(jnp.float32) * conv).astype(jnp.bfloat16)
    all_gated = lax.all_gather(gated, ("chan", "sub"), axis=1, tiled=True)
    mixed = jnp.dot(
        all_gated,
        lax.all_gather(out_weight, "ctx", axis=0, tiled=True),
        preferred_element_type=jnp.float32,
    )
    return mixed.astype(jnp.bfloat16)


def swap(value, *axes):
    sizes = [lax.axis_size(axis) for axis in axes]
    total = math.prod(sizes)
    flip, stride = 0, 1
    for size in reversed(sizes):
        flip += stride
        stride *= size
    return lax.ppermute(value, axes, [(i, i ^ flip) for i in range(total)])


def across(value, distance):
    count = lax.axis_size("ctx")
    return lax.ppermute(value, "ctx", [(i, i ^ distance) for i in range(count)])


VMEM = pl.BlockSpec(memory_space=pltpu.VMEM)


def local_call(kernel, out_shapes, *operands, scratch=(), flops=0):
    moved = sum(math.prod(o.shape) * o.dtype.itemsize for o in operands)
    return pl.pallas_call(
        kernel,
        out_shape=[jax.ShapeDtypeStruct(shape, jnp.bfloat16) for shape in out_shapes],
        in_specs=[VMEM] * len(operands),
        out_specs=[VMEM] * len(out_shapes),
        scratch_shapes=list(scratch),
        compiler_params=pltpu.CompilerParams(vmem_limit_bytes=16 * 2**20),
        cost_estimate=pl.CostEstimate(flops=flops, bytes_accessed=moved, transcendentals=0),
    )(*operands)


def where_am_i():
    z, x = lax.axis_index("ctx"), lax.axis_index("chan")
    pair, bit = z // 2, z % 2
    return z, x, pair, bit


def span(index, size):
    return pl.ds(pl.multiple_of(index * size, size), size)


def gated_kernel(place, row_ref, *refs):
    pieces, outs, padded, gates = refs[:4], refs[4:6], refs[6], refs[7]
    _, block, width = pieces[0].shape
    groups, span = row_ref.shape
    per_group = width // groups
    padded[0] = jnp.zeros((block, width), padded.dtype)
    padded[1] = jnp.zeros((block, width), padded.dtype)
    for distance in range(4):
        token = place[0] ^ distance
        padded[2 + token] = pieces[distance][0]
        gates[token] = pieces[distance][1]
    for group in range(groups):
        columns = pl.ds(group * per_group, per_group)
        rows = jnp.broadcast_to(row_ref[group : group + 1, :], (block, span))
        toeplitz = pltpu.roll(rows, 0, 1, stride=1, stride_axis=0).astype(jnp.bfloat16)
        for out_ref, pair in zip(outs, (1 - place[4], place[4])):
            for part in range(2):
                token = 2 * pair + part
                source = jnp.concatenate(
                    [padded[token + step, :, columns] for step in range(3)], axis=0
                )
                conv = jnp.dot(toeplitz, source, preferred_element_type=jnp.float32)
                gated = gates[token, :, columns].astype(jnp.float32) * conv
                out_ref[pl.ds(part * block, block), columns] = gated.astype(out_ref.dtype)


def gated_conv(place, first_rows, pieces):
    _, block, width = pieces[0].shape
    return pl.pallas_call(
        gated_kernel,
        out_shape=[jax.ShapeDtypeStruct((2 * block, width), jnp.bfloat16)] * 2,
        grid_spec=pltpu.PrefetchScalarGridSpec(
            num_scalar_prefetch=1,
            grid=(1,),
            in_specs=[pl.BlockSpec(first_rows.shape, lambda i, s: (0, 0))]
            + [pl.BlockSpec((2, block, width), lambda i, s: (0, 0, 0))] * 4,
            out_specs=[pl.BlockSpec((2 * block, width), lambda i, s: (0, 0))] * 2,
            scratch_shapes=[
                pltpu.VMEM((6, block, width), jnp.bfloat16),
                pltpu.VMEM((4, block, width), jnp.bfloat16),
            ],
        ),
        compiler_params=pltpu.CompilerParams(vmem_limit_bytes=16 * 2**20),
        cost_estimate=pl.CostEstimate(
            flops=2 * 4 * block * 3 * block * width, bytes_accessed=2**21, transcendentals=0
        ),
    )(place, first_rows, *pieces)


def project_kernel(place, *refs):
    mine, other, own_w, near_w, far_w, out_ref = refs[:4], *refs[4:9]
    bit, quarter, same, group = place[1], place[2], place[3], place[5]
    tokens, width = mine[0].shape
    half = tokens // 2
    columns = near_w.shape[1]
    for part in range(2):
        rows = pl.ds(part * half, half)
        for got_w, index in ((near_w, group), (far_w, 1 - group)):
            place_of = pl.ds(pl.multiple_of(index * columns, columns), columns)
            total = jnp.zeros((half, columns), jnp.float32)
            for flip in range(4):
                here, there = mine[flip][rows, :], other[flip, rows, :]
                first = jnp.where(same == 1, here, there)
                second = jnp.where(same == 1, there, here)
                block = pl.ds(pl.multiple_of((quarter ^ flip) * width, width), width)
                total += jnp.dot(first, own_w[block, place_of], preferred_element_type=jnp.float32)
                total += jnp.dot(second, got_w[block, :], preferred_element_type=jnp.float32)
            out_ref[part ^ bit, :, place_of] = total.astype(out_ref.dtype)


def project(place, mine, other, out_weight, near_w, far_w):
    tokens, width = mine[0].shape
    depth, columns = near_w.shape
    return pl.pallas_call(
        project_kernel,
        out_shape=jax.ShapeDtypeStruct((2, tokens // 2, 2 * columns), jnp.bfloat16),
        grid_spec=pltpu.PrefetchScalarGridSpec(
            num_scalar_prefetch=1,
            grid=(1,),
            in_specs=[pl.BlockSpec((tokens, width), lambda i, s: (0, 0))] * 4
            + [
                pl.BlockSpec((4, tokens, width), lambda i, s: (0, 0, 0)),
                pl.BlockSpec((depth, 2 * columns), lambda i, s: (0, s[1])),
                pl.BlockSpec((depth, columns), lambda i, s: (0, 0)),
                pl.BlockSpec((depth, columns), lambda i, s: (0, 0)),
            ],
            out_specs=pl.BlockSpec((2, tokens // 2, 2 * columns), lambda i, s: (0, 0, 0)),
        ),
        compiler_params=pltpu.CompilerParams(vmem_limit_bytes=16 * 2**20),
        cost_estimate=pl.CostEstimate(
            flops=2 * tokens * 8 * width * 2 * columns, bytes_accessed=2**22, transcendentals=0
        ),
    )(place, *mine, other, out_weight, near_w, far_w)


def project_whole_kernel(slots, *refs):
    outs, refs = refs[-len(slots) :], refs[: -len(slots)]
    mine, others, (own_w, near_w, far_w) = refs[:4], refs[4:-3], refs[-3:]
    if len(others) == 1:
        others = [others[0].at[flip] for flip in range(4)]
    _, x, _, bit = where_am_i()
    group, same = lax.axis_index("group"), lax.axis_index("sub") == bit
    tokens, width = mine[0].shape
    half = tokens // 2
    columns = near_w.shape[1]
    blocks = [span((2 * x + bit) ^ flip, width) for flip in range(4)]

    def fill(first, second):
        for got_w, index in ((near_w, group), (far_w, 1 - group)):
            place = span(2 * bit + index, columns)
            own_part = jnp.concatenate([own_w[block, place] for block in blocks], axis=0)
            got_part = jnp.concatenate([got_w[block, :] for block in blocks], axis=0)
            for slot, out_ref in zip(slots, outs):
                rows = span(slot ^ bit, half)
                total = jnp.dot(
                    jnp.concatenate([ref[rows, :] for ref in first], axis=1),
                    own_part,
                    preferred_element_type=jnp.float32,
                )
                total += jnp.dot(
                    jnp.concatenate([ref[rows, :] for ref in second], axis=1),
                    got_part,
                    preferred_element_type=jnp.float32,
                )
                out_ref[:, span(index, columns)] = total.astype(out_ref.dtype)

    @pl.when(same)
    def _():
        fill(mine, others)

    @pl.when(jnp.logical_not(same))
    def _():
        fill(others, mine)


def paired_plan(q_proj, k_proj, v_proj, filters, filter_blocks, out_weight):
    block, channels = q_proj.shape
    groups = filters.shape[0]
    g, z = lax.axis_index("group"), lax.axis_index("ctx")
    x, c = lax.axis_index("chan"), lax.axis_index("sub")
    pair, bit = z // 2, z % 2
    quarter = 2 * x + bit
    half, fourth = channels // 2, channels // 4
    place = jnp.stack([z, bit, quarter, (c == bit).astype(jnp.int32), pair, g]).astype(jnp.int32)

    def packed(quarter_index):
        k, v, q = (
            lax.dynamic_slice_in_dim(array, quarter_index * fourth, fourth, 1)
            for array in (k_proj, v_proj, q_proj)
        )
        product = (k.astype(jnp.float32) * v.astype(jnp.float32)).astype(jnp.bfloat16)
        return jnp.stack([product, q])

    tap_index = jnp.arange(filters.shape[1], dtype=jnp.int32)
    masked = jnp.where(tap_index[None, :] < filter_blocks[:, None] * block, filters, 0.0)
    masked = masked.astype(jnp.bfloat16)
    taken = groups // 4
    for_other = lax.dynamic_slice_in_dim(masked, (2 * (1 - x) + bit) * taken, taken, 0)
    filter_rows = for_other.reshape(-1, fourth)
    filter_rows = jnp.concatenate(
        [filter_rows, jnp.zeros((16 - filter_rows.shape[0], fourth), jnp.bfloat16)], axis=0
    )

    same_send = packed(2 * (1 - x) + bit)
    k_proj, v_proj, q_proj, same_send = lax.optimization_barrier((k_proj, v_proj, q_proj, same_send))
    flip_send = jnp.concatenate(
        [packed(2 * (1 - x) + 1 - bit).reshape(2 * block, fourth), filter_rows], axis=0
    )
    same_came = swap(same_send, "chan")
    flip_came = swap(flip_send, "chan")
    same_own, flip_own = packed(2 * x + bit), packed(2 * x + 1 - bit)

    other_cols = (1 - bit) * half + g * fourth
    w_near = across(lax.dynamic_slice_in_dim(out_weight, other_cols, fourth, 1), 1)
    w_far = swap(w_near, "group")

    inside = pair == x
    piece_2 = across(jnp.where(inside, same_came, same_own), 2)
    piece_0 = jnp.where(inside, same_own, same_came)
    flip_came_pieces = flip_came[: 2 * block].reshape(2, block, fourth)
    piece_3 = across(jnp.where(inside, flip_came_pieces, flip_own), 3)
    piece_1 = across(jnp.where(inside, flip_own, flip_came_pieces), 1)

    taps = jnp.where(
        inside,
        lax.dynamic_slice_in_dim(masked, quarter * taken, taken, 0),
        flip_came[2 * block :].reshape(-1)[: taken * filters.shape[1]].reshape(taken, -1),
    ).astype(jnp.float32)
    first_rows = jnp.concatenate(
        [jnp.zeros((taken, 1), jnp.float32), taps[:, ::-1], jnp.zeros((taken, block - 1), jnp.float32)],
        axis=1,
    )
    first_rows, w_near, w_far = lax.optimization_barrier((first_rows, w_near, w_far))
    gated_far, gated_near = gated_conv(place, first_rows, (piece_0, piece_1, piece_2, piece_3))

    def gathered(gated):
        return [gated, swap(gated, "ctx"), swap(gated, "chan"), swap(gated, "ctx", "chan")]

    def project(mine, other, slots=(0, 1)):
        return local_call(
            functools.partial(project_whole_kernel, slots), [(block, half)] * len(slots),
            *mine, *other, out_weight, w_near, w_far,
            flops=2 * block * channels * half * len(slots),
        )

    def partials(mine):
        other = swap(jnp.stack(mine), "sub")
        return project(mine, [other])

    far = partials(gathered(gated_far))
    far_own, far_near = across(far[0], 2), across(far[1], 3)

    def close_partials(mine):
        gated, beside, cross = mine
        crossed = swap(beside, "chan")
        mine = [*mine, crossed]
        other = swap(jnp.stack(mine), "sub")
        near = across(project(mine, [other], (1,))[0], 1)
        return project(mine, [other], (0,))[0], near

    def no_taps(mine):
        zeros = jnp.zeros((block, half), jnp.bfloat16)
        return zeros, zeros

    close_own, near = lax.cond(
        jnp.max(filter_blocks) > 0, close_partials, no_taps,
        [gated_near, swap(gated_near, "ctx"), swap(gated_near, "chan")],
    )
    this_half = close_own.astype(jnp.float32) + far_own.astype(jnp.float32)
    that_half = near.astype(jnp.float32) + far_near.astype(jnp.float32)
    left = jnp.where(bit == 0, this_half, that_half)
    right = jnp.where(bit == 0, that_half, this_half)
    return jnp.concatenate([left, right], axis=1).astype(jnp.bfloat16)


def solution(mesh):
    sizes = dict(mesh.shape)

    def per_device(q_proj, k_proj, v_proj, filters, filter_blocks, out_weight):
        block, channels = q_proj.shape
        groups, taps = filters.shape
        paired = (
            (sizes["group"], sizes["ctx"], sizes["chan"], sizes["sub"]) == (2, 4, 2, 2)
            and taps == 2 * block
            and taps == channels // 2
            and groups % 4 == 0
            and (channels // groups) % 128 == 0
            and out_weight.shape == (channels, channels)
        )
        plan = paired_plan if paired else gathered_plan
        return plan(q_proj, k_proj, v_proj, filters, filter_blocks, out_weight)

    in_specs = (
        P(("group", "ctx"), ("chan", "sub")),
        P(("group", "ctx"), ("chan", "sub")),
        P(("group", "ctx"), ("chan", "sub")),
        P(("chan", "sub"), None),
        P(("chan", "sub")),
        P("ctx", ("chan", "sub")),
    )
    out_specs = P(("group", "ctx"), ("chan", "sub"))
    return jax.shard_map(
        per_device, mesh=mesh, in_specs=in_specs, out_specs=out_specs, check_vma=False
    )
```

```python
import functools
import math

import jax
import jax.numpy as jnp
from jax import lax
from jax.experimental import pallas as pl
from jax.experimental.pallas import tpu as pltpu
from jax.sharding import PartitionSpec as P


def shifted(value, axis, steps):
    count = lax.axis_size(axis)
    leading, last = (max(0, -steps), min(count, count - steps))
    return lax.ppermute(value, axis, [(source, source + steps) for source in range(leading, last)])


def forward_table(block_len, columns):
    length = 2 * block_len
    frequency = jnp.arange(block_len, dtype=jnp.int32)[:, None]
    positions = jnp.arange(columns, dtype=jnp.int32)[None, :]
    angles = (frequency * positions % length).astype(jnp.float32) * (2.0 * math.pi / length)
    alternating = (1 - 2 * (positions % 2)).astype(jnp.float32)
    upper = jnp.cos(angles)
    bottom = jnp.where(frequency == 0, alternating, -jnp.sin(angles))
    return jnp.concatenate([upper, bottom], axis=0)


def inverse_table(block_len):
    length = 2 * block_len
    samples = jnp.arange(block_len, dtype=jnp.int32)[:, None]
    frequency = jnp.arange(block_len, dtype=jnp.int32)[None, :]
    angles = (frequency * samples % length).astype(jnp.float32) * (2.0 * math.pi / length)
    alternating = (1 - 2 * (samples % 2)).astype(jnp.float32)
    left_half = jnp.where(frequency == 0, 1.0, 2.0 * jnp.cos(angles)) / length
    right_half = jnp.where(frequency == 0, alternating, -2.0 * jnp.sin(angles)) / length
    return jnp.concatenate([left_half, right_half], axis=1)


def packed_product(filter_spec, data_spec, first_row, block_len):
    filt_re = filter_spec[:block_len]
    filt_im = filter_spec[block_len:]
    data_re = data_spec[:block_len]
    data_im = data_spec[block_len:]
    other_rows = 1.0 - first_row
    upper = filt_re * data_re - filt_im * data_im * other_rows
    bottom = (filt_re * data_im + filt_im * data_re) * other_rows + filt_im * data_im * first_row
    return jnp.concatenate([upper, bottom], axis=0)


def gathered_plan(q_proj, k_proj, v_proj, filters, filter_blocks, out_weight):
    block_len, channels = q_proj.shape
    groups = filters.shape[0]
    per_group = channels // groups
    reach = lax.axis_size("ctx") // 2
    highest = lax.Precision.HIGHEST
    product = (k_proj.astype(jnp.float32) * v_proj.astype(jnp.float32)).astype(jnp.bfloat16)
    tap_index = jnp.arange(filters.shape[1], dtype=jnp.int32)
    masked = jnp.where(tap_index[None, :] < filter_blocks[:, None] * block_len, filters, 0.0)
    tap_blocks = masked.reshape(groups, reach, block_len)
    empty_block = jnp.zeros((groups, 1, block_len), jnp.float32)
    extended = jnp.concatenate([empty_block, tap_blocks, empty_block], axis=1)
    segments = jnp.concatenate([extended[:, 1:], extended[:, :-1]], axis=2)
    full_table = forward_table(block_len, 2 * block_len)
    filter_spectra = jnp.einsum("gdm,fm->dfg", segments, full_table, precision=highest)
    half_table = forward_table(block_len, block_len)
    table_high = half_table.astype(jnp.bfloat16)
    table_low = (half_table - table_high.astype(jnp.float32)).astype(jnp.bfloat16)
    first_row = (jnp.arange(block_len) == 0).astype(jnp.float32)[:, None, None]
    longest = jnp.max(filter_blocks)
    position = lax.axis_index("ctx")

    def transform(block):
        spectrum = jnp.dot(table_high, block, preferred_element_type=jnp.float32)
        spectrum = spectrum + jnp.dot(table_low, block, preferred_element_type=jnp.float32)
        return spectrum.reshape(2 * block_len, groups, per_group)

    def contribution(running, block, distance):
        filter_spec = lax.dynamic_index_in_dim(filter_spectra, distance, 0, keepdims=False)[
            :, :, None
        ]

        def add_term(partial_sum):
            return partial_sum + packed_product(filter_spec, transform(block), first_row, block_len)

        needed = (distance <= longest) & (position >= distance)
        return lax.cond(needed, add_term, lambda partial_sum: partial_sum, running)

    running = packed_product(
        filter_spectra[0][:, :, None], transform(product), first_row, block_len
    )

    def relay_step(distance, carry):
        carried, partial_sum = carry
        carried = shifted(carried, "ctx", 1)
        return (carried, contribution(partial_sum, carried, distance))

    carried, running = lax.fori_loop(1, reach + 1, relay_step, (product, running))
    spectrum_sum = running.reshape(2 * block_len, channels)
    conv = jnp.dot(inverse_table(block_len), spectrum_sum, precision=highest)
    gated = (q_proj.astype(jnp.float32) * conv).astype(jnp.bfloat16)
    all_gated = lax.all_gather(gated, ("chan", "sub"), axis=1, tiled=True)
    mixed = jnp.dot(
        all_gated,
        lax.all_gather(out_weight, "ctx", axis=0, tiled=True),
        preferred_element_type=jnp.float32,
    )
    return mixed.astype(jnp.bfloat16)


def swap(value, *axes):
    sizes = [lax.axis_size(axis) for axis in axes]
    total = math.prod(sizes)
    flip, stride = 0, 1
    for size in reversed(sizes):
        flip += stride
        stride *= size
    return lax.ppermute(value, axes, [(i, i ^ flip) for i in range(total)])


def across(value, distance):
    count = lax.axis_size("ctx")
    return lax.ppermute(value, "ctx", [(i, i ^ distance) for i in range(count)])


VMEM = pl.BlockSpec(memory_space=pltpu.VMEM)


def local_call(kernel, out_shapes, *operands, scratch=(), flops=0):
    moved = sum(math.prod(o.shape) * o.dtype.itemsize for o in operands)
    return pl.pallas_call(
        kernel,
        out_shape=[jax.ShapeDtypeStruct(shape, jnp.bfloat16) for shape in out_shapes],
        in_specs=[VMEM] * len(operands),
        out_specs=[VMEM] * len(out_shapes),
        scratch_shapes=list(scratch),
        compiler_params=pltpu.CompilerParams(vmem_limit_bytes=16 * 2**20),
        cost_estimate=pl.CostEstimate(flops=flops, bytes_accessed=moved, transcendentals=0),
    )(*operands)


def where_am_i():
    z, x = lax.axis_index("ctx"), lax.axis_index("chan")
    pair, bit = z // 2, z % 2
    return z, x, pair, bit


def span(index, size):
    return pl.ds(pl.multiple_of(index * size, size), size)


def gated_kernel(place, row_ref, *refs):
    pieces, outs, padded, gates = refs[:4], refs[4:6], refs[6], refs[7]
    _, block, width = pieces[0].shape
    groups, span = row_ref.shape
    per_group = width // groups
    padded[0] = jnp.zeros((block, width), padded.dtype)
    padded[1] = jnp.zeros((block, width), padded.dtype)
    for distance in range(4):
        token = place[0] ^ distance
        padded[2 + token] = pieces[distance][0]
        gates[token] = pieces[distance][1]
    for group in range(groups):
        columns = pl.ds(group * per_group, per_group)
        rows = jnp.broadcast_to(row_ref[group : group + 1, :], (block, span))
        toeplitz = pltpu.roll(rows, 0, 1, stride=1, stride_axis=0).astype(jnp.bfloat16)
        for out_ref, pair in zip(outs, (1 - place[4], place[4])):
            for part in range(2):
                token = 2 * pair + part
                source = jnp.concatenate(
                    [padded[token + step, :, columns] for step in range(3)], axis=0
                )
                conv = jnp.dot(toeplitz, source, preferred_element_type=jnp.float32)
                gated = gates[token, :, columns].astype(jnp.float32) * conv
                out_ref[pl.ds(part * block, block), columns] = gated.astype(out_ref.dtype)


def gated_conv(place, first_rows, pieces):
    _, block, width = pieces[0].shape
    return pl.pallas_call(
        gated_kernel,
        out_shape=[jax.ShapeDtypeStruct((2 * block, width), jnp.bfloat16)] * 2,
        grid_spec=pltpu.PrefetchScalarGridSpec(
            num_scalar_prefetch=1,
            grid=(1,),
            in_specs=[pl.BlockSpec(first_rows.shape, lambda i, s: (0, 0))]
            + [pl.BlockSpec((2, block, width), lambda i, s: (0, 0, 0))] * 4,
            out_specs=[pl.BlockSpec((2 * block, width), lambda i, s: (0, 0))] * 2,
            scratch_shapes=[
                pltpu.VMEM((6, block, width), jnp.bfloat16),
                pltpu.VMEM((4, block, width), jnp.bfloat16),
            ],
        ),
        compiler_params=pltpu.CompilerParams(vmem_limit_bytes=16 * 2**20),
        cost_estimate=pl.CostEstimate(
            flops=2 * 4 * block * 3 * block * width, bytes_accessed=2**21, transcendentals=0
        ),
    )(place, first_rows, *pieces)


def project_kernel(place, *refs):
    mine, other, own_w, near_w, far_w, out_ref = refs[:4], *refs[4:9]
    bit, quarter, same, group = place[1], place[2], place[3], place[5]
    tokens, width = mine[0].shape
    half = tokens // 2
    columns = near_w.shape[1]
    for part in range(2):
        rows = pl.ds(part * half, half)
        for got_w, index in ((near_w, group), (far_w, 1 - group)):
            place_of = pl.ds(pl.multiple_of(index * columns, columns), columns)
            total = jnp.zeros((half, columns), jnp.float32)
            for flip in range(4):
                here, there = mine[flip][rows, :], other[flip, rows, :]
                first = jnp.where(same == 1, here, there)
                second = jnp.where(same == 1, there, here)
                block = pl.ds(pl.multiple_of((quarter ^ flip) * width, width), width)
                total += jnp.dot(first, own_w[block, place_of], preferred_element_type=jnp.float32)
                total += jnp.dot(second, got_w[block, :], preferred_element_type=jnp.float32)
            out_ref[part ^ bit, :, place_of] = total.astype(out_ref.dtype)


def project(place, mine, other, out_weight, near_w, far_w):
    tokens, width = mine[0].shape
    depth, columns = near_w.shape
    return pl.pallas_call(
        project_kernel,
        out_shape=jax.ShapeDtypeStruct((2, tokens // 2, 2 * columns), jnp.bfloat16),
        grid_spec=pltpu.PrefetchScalarGridSpec(
            num_scalar_prefetch=1,
            grid=(1,),
            in_specs=[pl.BlockSpec((tokens, width), lambda i, s: (0, 0))] * 4
            + [
                pl.BlockSpec((4, tokens, width), lambda i, s: (0, 0, 0)),
                pl.BlockSpec((depth, 2 * columns), lambda i, s: (0, s[1])),
                pl.BlockSpec((depth, columns), lambda i, s: (0, 0)),
                pl.BlockSpec((depth, columns), lambda i, s: (0, 0)),
            ],
            out_specs=pl.BlockSpec((2, tokens // 2, 2 * columns), lambda i, s: (0, 0, 0)),
        ),
        compiler_params=pltpu.CompilerParams(vmem_limit_bytes=16 * 2**20),
        cost_estimate=pl.CostEstimate(
            flops=2 * tokens * 8 * width * 2 * columns, bytes_accessed=2**22, transcendentals=0
        ),
    )(place, *mine, other, out_weight, near_w, far_w)


def project_whole_kernel(slots, *refs):
    outs, refs = refs[-len(slots) :], refs[: -len(slots)]
    mine, others, (own_w, near_w, far_w) = refs[:4], refs[4:-3], refs[-3:]
    if len(others) == 1:
        others = [others[0].at[flip] for flip in range(4)]
    _, x, _, bit = where_am_i()
    group, same = lax.axis_index("group"), lax.axis_index("sub") == bit
    tokens, width = mine[0].shape
    half = tokens // 2
    columns = near_w.shape[1]
    blocks = [span((2 * x + bit) ^ flip, width) for flip in range(4)]

    def fill(first, second):
        for got_w, index in ((near_w, group), (far_w, 1 - group)):
            place = span(2 * bit + index, columns)
            own_part = jnp.concatenate([own_w[block, place] for block in blocks], axis=0)
            got_part = jnp.concatenate([got_w[block, :] for block in blocks], axis=0)
            for slot, out_ref in zip(slots, outs):
                rows = span(slot ^ bit, half)
                total = jnp.dot(
                    jnp.concatenate([ref[rows, :] for ref in first], axis=1),
                    own_part,
                    preferred_element_type=jnp.float32,
                )
                total += jnp.dot(
                    jnp.concatenate([ref[rows, :] for ref in second], axis=1),
                    got_part,
                    preferred_element_type=jnp.float32,
                )
                out_ref[:, span(index, columns)] = total.astype(out_ref.dtype)

    @pl.when(same)
    def _():
        fill(mine, others)

    @pl.when(jnp.logical_not(same))
    def _():
        fill(others, mine)


def paired_plan(q_proj, k_proj, v_proj, filters, filter_blocks, out_weight):
    block, channels = q_proj.shape
    groups = filters.shape[0]
    g, z = lax.axis_index("group"), lax.axis_index("ctx")
    x, c = lax.axis_index("chan"), lax.axis_index("sub")
    pair, bit = z // 2, z % 2
    quarter = 2 * x + bit
    half, fourth = channels // 2, channels // 4
    place = jnp.stack([z, bit, quarter, (c == bit).astype(jnp.int32), pair, g]).astype(jnp.int32)

    def packed(quarter_index):
        k, v, q = (
            lax.dynamic_slice_in_dim(array, quarter_index * fourth, fourth, 1)
            for array in (k_proj, v_proj, q_proj)
        )
        product = (k.astype(jnp.float32) * v.astype(jnp.float32)).astype(jnp.bfloat16)
        return jnp.stack([product, q])

    tap_index = jnp.arange(filters.shape[1], dtype=jnp.int32)
    masked = jnp.where(tap_index[None, :] < filter_blocks[:, None] * block, filters, 0.0)
    masked = masked.astype(jnp.bfloat16)
    taken = groups // 4
    for_other = lax.dynamic_slice_in_dim(masked, (2 * (1 - x) + bit) * taken, taken, 0)
    filter_rows = for_other.reshape(-1, fourth)
    filter_rows = jnp.concatenate(
        [filter_rows, jnp.zeros((16 - filter_rows.shape[0], fourth), jnp.bfloat16)], axis=0
    )

    other_cols = (1 - bit) * half + g * fourth
    w_send = lax.dynamic_slice_in_dim(out_weight, other_cols, fourth, 1)
    same_send = packed(2 * (1 - x) + bit)
    k_proj, v_proj, q_proj, same_send, w_send = lax.optimization_barrier(
        (k_proj, v_proj, q_proj, same_send, w_send)
    )
    flip_send = jnp.concatenate(
        [packed(2 * (1 - x) + 1 - bit).reshape(2 * block, fourth), filter_rows], axis=0
    )
    same_came = swap(same_send, "chan")
    flip_came = swap(flip_send, "chan")
    same_own, flip_own = packed(2 * x + bit), packed(2 * x + 1 - bit)

    w_near = across(w_send, 1)
    w_far = swap(w_near, "group")

    inside = pair == x
    piece_2 = across(jnp.where(inside, same_came, same_own), 2)
    piece_0 = jnp.where(inside, same_own, same_came)
    flip_came_pieces = flip_came[: 2 * block].reshape(2, block, fourth)
    piece_3 = across(jnp.where(inside, flip_came_pieces, flip_own), 3)
    piece_1 = across(jnp.where(inside, flip_own, flip_came_pieces), 1)

    taps = jnp.where(
        inside,
        lax.dynamic_slice_in_dim(masked, quarter * taken, taken, 0),
        flip_came[2 * block :].reshape(-1)[: taken * filters.shape[1]].reshape(taken, -1),
    ).astype(jnp.float32)
    first_rows = jnp.concatenate(
        [jnp.zeros((taken, 1), jnp.float32), taps[:, ::-1], jnp.zeros((taken, block - 1), jnp.float32)],
        axis=1,
    )
    first_rows, w_near, w_far = lax.optimization_barrier((first_rows, w_near, w_far))
    gated_far, gated_near = gated_conv(place, first_rows, (piece_0, piece_1, piece_2, piece_3))

    def gathered(gated):
        return [gated, swap(gated, "ctx"), swap(gated, "chan"), swap(gated, "ctx", "chan")]

    def project(mine, other, slots=(0, 1)):
        return local_call(
            functools.partial(project_whole_kernel, slots), [(block, half)] * len(slots),
            *mine, *other, out_weight, w_near, w_far,
            flops=2 * block * channels * half * len(slots),
        )

    def partials(mine):
        other = swap(jnp.stack(mine), "sub")
        return project(mine, [other])

    far = partials(gathered(gated_far))
    far_own, far_near = across(far[0], 2), across(far[1], 3)

    def close_partials(mine):
        gated, beside, cross = mine
        crossed = swap(beside, "chan")
        mine = [*mine, crossed]
        other = swap(jnp.stack(mine), "sub")
        near = across(project(mine, [other], (1,))[0], 1)
        return project(mine, [other], (0,))[0], near

    def no_taps(mine):
        zeros = jnp.zeros((block, half), jnp.bfloat16)
        return zeros, zeros

    close_own, near = lax.cond(
        jnp.max(filter_blocks) > 0, close_partials, no_taps,
        [gated_near, swap(gated_near, "ctx"), swap(gated_near, "chan")],
    )
    this_half = close_own.astype(jnp.float32) + far_own.astype(jnp.float32)
    that_half = near.astype(jnp.float32) + far_near.astype(jnp.float32)
    left = jnp.where(bit == 0, this_half, that_half)
    right = jnp.where(bit == 0, that_half, this_half)
    return jnp.concatenate([left, right], axis=1).astype(jnp.bfloat16)


def solution(mesh):
    sizes = dict(mesh.shape)

    def per_device(q_proj, k_proj, v_proj, filters, filter_blocks, out_weight):
        block, channels = q_proj.shape
        groups, taps = filters.shape
        paired = (
            (sizes["group"], sizes["ctx"], sizes["chan"], sizes["sub"]) == (2, 4, 2, 2)
            and taps == 2 * block
            and taps == channels // 2
            and groups % 4 == 0
            and (channels // groups) % 128 == 0
            and out_weight.shape == (channels, channels)
        )
        plan = paired_plan if paired else gathered_plan
        return plan(q_proj, k_proj, v_proj, filters, filter_blocks, out_weight)

    in_specs = (
        P(("group", "ctx"), ("chan", "sub")),
        P(("group", "ctx"), ("chan", "sub")),
        P(("group", "ctx"), ("chan", "sub")),
        P(("chan", "sub"), None),
        P(("chan", "sub")),
        P("ctx", ("chan", "sub")),
    )
    out_specs = P(("group", "ctx"), ("chan", "sub"))
    return jax.shard_map(
        per_device, mesh=mesh, in_specs=in_specs, out_specs=out_specs, check_vma=False
    )
```
